512 devices in a mesh: district: 16 (over y, core), tile: 32 (over z, x).
Axes of the slice: x: 4, y: 8, z: 8, core: 2. Of those that a mesh axis runs over, the one named last changes fastest.
Arguments:
- features: bfloat16 [2048, 96, 128], P(('district', 'tile')), may hold values from -6 to 6
- pre_act: bfloat16 [2048, 96, 128], P(('district', 'tile')), may hold values from -6 to 6
- out_grad: bfloat16 [2048, 96, 128], P(('district', 'tile')), may hold values from -6 to 6
- weight_one: bfloat16 [27, 96, 96], replicated, may hold values from -0.15625 to 0.15625
- weight_two: bfloat16 [27, 96, 96], replicated, may hold values from -0.15625 to 0.15625
- block_count: int32 [512], P(('district', 'tile')), may hold values from 1 to 4, as said below
- pair_in: int32 [512, 64], P(('district', 'tile')), may hold values from 0 to 11, as said below
- pair_off: int32 [512, 64], P(('district', 'tile')), may hold values from 0 to 26
- row_map: int32 [512, 64, 128], P(('district', 'tile')), may hold values from 0 to 159
- send_lo: int32 [512, 4], P(('district', 'tile')), may hold values from 0 to 3, as said below
- send_hi: int32 [512, 4], P(('district', 'tile')), may hold values from 0 to 3, as said below
Outputs:
- feature_grad: bfloat16 [2048, 96, 128], P(('district', 'tile'))
- grad_one: float32 [27, 96, 96], replicated
- grad_two: float32 [27, 96, 96], replicated
The draws below stay inside these ranges and needn't reach their ends.
Inputs may be any that keep to these rules, and one draw needn't show every extreme that they name: `block_count`: at most 4, reached by some tile in every draw; at least 1. `pair_in`: an index of the tile's extended list: below its block_count (own blocks), or 4 to 11. `row_map`: values of 128 or more mean no input voxel. `send_lo`: active blocks of the sending tile, below its block_count; repeats possible. `send_hi`: active blocks of the sending tile, below its block_count; repeats possible.
All inputs are finite; a program needn't handle non-finite values.
Results may differ from the reference program's by a relative error of at most 0.0049.
Values may be sent and summed in bfloat16 or wider, within the bound.
A program may use at most 64 MiB of HBM per device.

```python
import jax
import jax.numpy as jnp
from jax import lax

C = 96
NB = 4
ROW = 128
K = 27
PB = 16
KB = 4
P_SIZE = 64
BLOCKS = 2048
N_DISTRICT = 16
N_TILE = 32
DEVICES = 512


def tile_active_count(key):
    lowest = max(1, NB // 3)
    counts = jax.random.randint(key, (DEVICES,), lowest, NB + 1, dtype=jnp.int32)
    chosen = jax.random.randint(jax.random.fold_in(key, 7), (), 0, DEVICES, dtype=jnp.int32)
    return counts.at[chosen].set(NB)


def draw_block_count(key, part):
    return tile_active_count(key)


def draw_pair_in(key, part):
    counts = tile_active_count(key)
    key = jax.random.fold_in(key, 11)
    raw = jax.random.randint(key, (DEVICES, P_SIZE), 0, 1 << 20, dtype=jnp.int32)
    picked = raw % (counts[:, None] + 2 * KB)
    return jnp.where(picked < counts[:, None], picked, NB + picked - counts[:, None]).astype(jnp.int32)


def draw_send_lo(key, part):
    counts = tile_active_count(key)
    key = jax.random.fold_in(key, 13)
    raw = jax.random.randint(key, (DEVICES, KB), 0, 1 << 20, dtype=jnp.int32)
    return (raw % counts[:, None]).astype(jnp.int32)


def draw_send_hi(key, part):
    counts = tile_active_count(key)
    key = jax.random.fold_in(key, 17)
    raw = jax.random.randint(key, (DEVICES, KB), 0, 1 << 20, dtype=jnp.int32)
    return (raw % counts[:, None]).astype(jnp.int32)


def set_ends(array, key, smallest, top_value):
    longest = array.shape.index(max(array.shape))
    spots = []
    for shift in (0, 1):
        where = [jax.random.randint(jax.random.fold_in(key, axis), (), 0, length) for axis, length in enumerate(array.shape)]
        where[longest] = (where[longest] + shift) % array.shape[longest]
        spots.append(tuple(where))
    return array.at[spots[0]].set(smallest).at[spots[1]].set(top_value)


def block_scale(rng, extent, split, least, largest):
    def one(dim, shards_of):
        heights = jax.random.uniform(jax.random.fold_in(jax.random.fold_in(rng, 6), dim), (shards_of,), jnp.float32, least / len(split), largest / len(split))
        return jnp.repeat(jnp.exp(heights), extent[dim] // shards_of).reshape((-1,) + (1,) * (len(extent) - dim - 1))

    factor_of = one(*split[0])
    for cut in split[1:]:
        factor_of = factor_of * one(*cut)
    return factor_of


def scatter_about(key, dims, spread, most, split=(), kind=jnp.bfloat16):
    loudness = block_scale(key, dims, split, -0.22, 0.18) if split else 1.0
    values = jax.random.normal(key, dims, jnp.float32) * spread * loudness
    return jnp.minimum(jnp.maximum(values, -most), most).astype(kind)


def setup_inputs(seed: int = 0) -> dict:
    key_list = jax.random.split(jax.random.key(seed), 12)
    return {
        "features": scatter_about(key_list[0], (BLOCKS, C, ROW), 1.0, 6.0, ((0, 512),)),
        "pre_act": scatter_about(key_list[1], (BLOCKS, C, ROW), 1.0, 6.0, ((0, 512),)),
        "out_grad": scatter_about(key_list[2], (BLOCKS, C, ROW), 1.0, 6.0, ((0, 512),)),
        "weight_one": scatter_about(key_list[3], (K, C, C), (PB * C) ** -0.5, 0.15625),
        "weight_two": scatter_about(key_list[4], (K, C, C), (PB * C) ** -0.5, 0.15625),
        "block_count": draw_block_count(jax.random.fold_in(key_list[11], 71), 0),
        "pair_in": draw_pair_in(jax.random.fold_in(key_list[11], 71), 0),
        "pair_off": set_ends(jax.random.randint(key_list[7], (DEVICES, P_SIZE), 0, K), jax.random.fold_in(key_list[7], 1), 0, K - 1).astype(jnp.int32),
        "row_map": set_ends(jax.random.randint(key_list[8], (DEVICES, P_SIZE, ROW), 0, ROW + ROW // 4), jax.random.fold_in(key_list[8], 1), 0, (ROW + ROW // 4) - 1).astype(jnp.int32),
        "send_lo": draw_send_lo(jax.random.fold_in(key_list[11], 71), 0),
        "send_hi": draw_send_hi(jax.random.fold_in(key_list[11], 71), 0),
    }


def build_ext(field, send_lo, send_hi):
    lower_part = jnp.take_along_axis(field, send_lo[:, :, None, None], axis=1)
    upper_part = jnp.take_along_axis(field, send_hi[:, :, None, None], axis=1)
    shape = (N_DISTRICT, N_TILE) + lower_part.shape[1:]
    lower_part = lower_part.reshape(shape)
    upper_part = upper_part.reshape(shape)
    blank = jnp.zeros_like(lower_part[:, :1])
    from_lower = jnp.concatenate([blank, upper_part[:, :-1]], axis=1).reshape((-1,) + shape[2:])
    from_upper = jnp.concatenate([lower_part[:, 1:], blank], axis=1).reshape((-1,) + shape[2:])
    return jnp.concatenate([field, from_lower, from_upper], axis=1)


def tile_layer(kernel_weight, item):
    ext, output_gradient, pin, pair_offset_table, rmap, count = item
    pidx = jnp.arange(P_SIZE, dtype=jnp.int32)
    live = (pidx // PB) < count
    valid = (rmap < ROW) & live[:, None]
    cols = jnp.where(rmap < ROW, rmap, 0).astype(jnp.int32)
    picked = ext[pin]
    gathered_input_rows = jnp.take_along_axis(picked, cols[:, None, :], axis=2)
    gathered_input_rows = jnp.where(valid[:, None, :], gathered_input_rows, jnp.zeros_like(gathered_input_rows))
    output_grad_pairs = output_gradient[pidx // PB]
    weight_grad_pairs = jnp.einsum("gmq,guq->gmu", gathered_input_rows.astype(jnp.float32), output_grad_pairs.astype(jnp.float32))
    dw_tile = jax.ops.segment_sum(weight_grad_pairs, pair_offset_table, num_segments=K)
    gathered_grad_rows = jnp.einsum("kly,kyz->klz", kernel_weight[pair_offset_table].astype(jnp.float32), output_grad_pairs.astype(jnp.float32))
    gathered_grad_rows = jnp.where(valid[:, None, :], gathered_grad_rows, 0.0)
    flat_idx = (pin[:, None] * ROW + cols).reshape(-1)
    chans = gathered_grad_rows.shape[1]
    total = jnp.zeros((chans, ext.shape[0] * ROW), jnp.float32)
    total = total.at[:, flat_idx].add(jnp.transpose(gathered_grad_rows, (1, 0, 2)).reshape(chans, -1))
    dext = jnp.transpose(total.reshape(chans, ext.shape[0], ROW), (1, 0, 2))
    return dext, dw_tile


def layer_back(ext, output_gradient, kernel_weight, counts, pair_in, pair_off, row_map, send_lo, send_hi):
    def step(carry, item):
        dext, dw_tile = tile_layer(kernel_weight, item)
        return carry + dw_tile, dext

    chans = kernel_weight.shape[1]
    init = jnp.zeros((K, chans, chans), jnp.float32)
    dw_all, dext = lax.scan(step, init, (ext, output_gradient, pair_in, pair_off, row_map, counts))
    local = dext[:, :NB]
    low = dext[:, NB:NB + KB]
    high = dext[:, NB + KB:]
    shape = (N_DISTRICT, N_TILE) + low.shape[1:]
    low = low.reshape(shape)
    high = high.reshape(shape)
    blank = jnp.zeros_like(low[:, :1])
    for_lo = jnp.concatenate([blank, high[:, :-1]], axis=1).reshape((-1,) + shape[2:])
    for_hi = jnp.concatenate([low[:, 1:], blank], axis=1).reshape((-1,) + shape[2:])

    def add_back(blocks, lo_idx, hi_idx, lo_val, hi_val):
        return blocks.at[lo_idx].add(lo_val).at[hi_idx].add(hi_val)

    local = jax.vmap(add_back)(local, send_lo, send_hi, for_lo, for_hi)
    return local, dw_all


def reference(features, pre_act, out_grad, weight_one, weight_two, block_count, pair_in, pair_off, row_map, send_lo, send_hi):
    chans = features.shape[1]
    shape = (-1, NB, chans, ROW)
    feat = features.reshape(shape)
    pre = pre_act.reshape(shape)
    gout = out_grad.reshape(shape)
    hidden = jnp.maximum(pre, jnp.zeros_like(pre))
    ext_x = build_ext(feat, send_lo, send_hi)
    ext_h = build_ext(hidden, send_lo, send_hi)
    hidden_grad, grad_two = layer_back(ext_h, gout, weight_two, block_count, pair_in, pair_off, row_map, send_lo, send_hi)
    act_grad = jnp.where(pre > 0, hidden_grad, 0.0).astype(jnp.bfloat16)
    feature_grad, grad_one = layer_back(ext_x, act_grad, weight_one, block_count, pair_in, pair_off, row_map, send_lo, send_hi)
    feature_grad = feature_grad.reshape(features.shape).astype(jnp.bfloat16)
    return feature_grad, grad_one, grad_two
```

```python
import functools

import jax
import jax.numpy as jnp
from jax import lax
from jax.experimental import pallas as pl
from jax.experimental.pallas import tpu as pltpu
from jax.sharding import PartitionSpec as P

K = 27
PB = 16
NB = 4
KB = 4
C = 96
ROW = 128
EXT = NB + 2 * KB
PACKED = 2048
F32 = jnp.float32
BF16 = jnp.bfloat16
VMEM_LIMIT = 32 * 1024 * 1024

SMEM = pl.BlockSpec(memory_space=pltpu.SMEM)
VMEM = pl.BlockSpec(memory_space=pltpu.VMEM)


def remote(src, dst, send_sem, recv_sem, where):
    return pltpu.make_async_remote_copy(
        src_ref=src,
        dst_ref=dst,
        send_sem=send_sem,
        recv_sem=recv_sem,
        device_id=where,
        device_id_type=pl.DeviceIdType.MESH,
    )


def greet(peers):
    barrier = pltpu.get_barrier_semaphore()
    for peer in peers:
        pl.semaphore_signal(barrier, inc=1, device_id=peer, device_id_type=pl.DeviceIdType.MESH)
    pl.semaphore_wait(barrier, len(peers))


def tile_neighbours():
    district = lax.axis_index("district")
    tile = lax.axis_index("tile")
    tiles = lax.axis_size("tile")
    below = (district, lax.rem(tile + tiles - 1, tiles))
    above = (district, lax.rem(tile + 1, tiles))
    has_below = tile > 0
    has_above = tile < tiles - 1
    return below, above, has_below, has_above


def halo_kernel(lo_ref, hi_ref, feat_ref, pre_ref, low_ref, high_ref, out_lo, out_hi, in_lo, in_hi, send, recv):
    below, above, has_below, has_above = tile_neighbours()
    greet((below, above))
    for j in range(KB):
        out_lo[0, j] = feat_ref[lo_ref[0, j]]
        out_lo[1, j] = jnp.maximum(pre_ref[lo_ref[0, j]], 0.0)
        out_hi[0, j] = feat_ref[hi_ref[0, j]]
        out_hi[1, j] = jnp.maximum(pre_ref[hi_ref[0, j]], 0.0)
    up = remote(out_hi, in_lo, send.at[0], recv.at[0], above)
    down = remote(out_lo, in_hi, send.at[1], recv.at[1], below)
    up.start()
    down.start()
    up.wait()
    low_ref[...] = jnp.where(has_below, in_lo[...], jnp.zeros_like(in_lo))
    down.wait()
    high_ref[...] = jnp.where(has_above, in_hi[...], jnp.zeros_like(in_hi))


def halo(send_lo, send_hi, features, pre_act):
    part = jax.ShapeDtypeStruct((2, KB, C, ROW), BF16)
    return pl.pallas_call(
        halo_kernel,
        out_shape=(part, part),
        in_specs=[SMEM, SMEM, VMEM, VMEM],
        out_specs=(VMEM, VMEM),
        scratch_shapes=[pltpu.VMEM((2, KB, C, ROW), BF16)] * 4
        + [pltpu.SemaphoreType.DMA((2,)), pltpu.SemaphoreType.DMA((2,))],
        compiler_params=pltpu.CompilerParams(
            collective_id=0, has_side_effects=True, vmem_limit_bytes=VMEM_LIMIT
        ),
        name="halo",
    )(send_lo, send_hi, features, pre_act)


def give_back_kernel(low_ref, high_ref, lo_ref, hi_ref, in_lo, in_hi, send, recv):
    below, above, has_below, has_above = tile_neighbours()
    greet((below, above))
    up = remote(high_ref, in_lo, send.at[0], recv.at[0], above)
    down = remote(low_ref, in_hi, send.at[1], recv.at[1], below)
    up.start()
    down.start()
    up.wait()
    lo_ref[...] = jnp.where(has_below, in_lo[...], jnp.zeros_like(in_lo))
    down.wait()
    hi_ref[...] = jnp.where(has_above, in_hi[...], jnp.zeros_like(in_hi))


def give_back(low, high):
    part = jax.ShapeDtypeStruct((KB, C, ROW), BF16)
    return pl.pallas_call(
        give_back_kernel,
        out_shape=(part, part),
        in_specs=[VMEM, VMEM],
        out_specs=(VMEM, VMEM),
        scratch_shapes=[pltpu.VMEM((KB, C, ROW), BF16)] * 2
        + [pltpu.SemaphoreType.DMA((2,)), pltpu.SemaphoreType.DMA((2,))],
        compiler_params=pltpu.CompilerParams(
            collective_id=1, has_side_effects=True, vmem_limit_bytes=VMEM_LIMIT
        ),
        name="give_back",
    )(low, high)


def layer_body(count_ref, pin_ref, poff_ref, rmap_ref, w_ref, ext, grad, dwp_ref, own_ref, low_ref, high_ref, dext, dw):
    dext[...] = jnp.zeros_like(dext)
    dw[...] = jnp.zeros_like(dw)
    rows = lax.broadcasted_iota(jnp.int32, (ROW, ROW), 0)

    def block(o, carry):
        maps = rmap_ref[0, pl.ds(pl.multiple_of(o * PB, PB), PB), :]
        g = grad[o]
        for j in range(PB):
            b = pin_ref[0, o * PB + j]
            k = poff_ref[0, o * PB + j]
            picks = jnp.where(rows == maps[j : j + 1, :], 1.0, 0.0).astype(BF16)
            ht = lax.dot_general(picks, g, (((1,), (1,)), ((), ())), preferred_element_type=F32).astype(BF16)
            dw[k, :, 0:C] += jnp.dot(ext[b], ht, preferred_element_type=F32)
            dext[b] += lax.dot_general(w_ref[k], ht, (((1,), (1,)), ((), ())), preferred_element_type=F32)
        return carry

    lax.fori_loop(0, count_ref[0], block, 0)
    own_ref[...] = dext[0:NB]
    low_ref[...] = dext[NB : NB + KB].astype(BF16)
    high_ref[...] = dext[NB + KB :].astype(BF16)
    lane = lax.broadcasted_iota(jnp.int32, (C, ROW), 1)
    for q in range(7):
        a = dw[4 * q]
        b = pltpu.roll(dw[4 * q + 1], 96, 1)
        c = pltpu.roll(dw[4 * q + 2], 64, 1)
        d = pltpu.roll(dw[4 * q + 3], 32, 1)
        base = q * 3 * C
        dwp_ref[base : base + C, :] = jnp.where(lane < 96, a, b)
        dwp_ref[base + C : base + 2 * C, :] = jnp.where(lane < 64, b, c)
        dwp_ref[base + 2 * C : base + 3 * C, :] = jnp.where(lane < 32, c, d)
    dwp_ref[21 * C :, :] = jnp.zeros((PACKED - 21 * C, ROW), F32)


def layer_two_kernel(count_ref, pin_ref, poff_ref, rmap_ref, w_ref, pre_ref, elow_ref, ehigh_ref, grad_ref,
                     dwp_ref, own_ref, low_ref, high_ref, ext, dext, dw):
    ext[0:NB] = jnp.maximum(pre_ref[...], 0.0)
    ext[NB : NB + KB] = elow_ref[1]
    ext[NB + KB :] = ehigh_ref[1]
    layer_body(count_ref, pin_ref, poff_ref, rmap_ref, w_ref, ext, grad_ref, dwp_ref, own_ref, low_ref, high_ref, dext, dw)


def layer_one_kernel(count_ref, pin_ref, poff_ref, rmap_ref, w_ref, feat_ref, elow_ref, ehigh_ref,
                     slo_ref, shi_ref, pre_ref, hown_ref, flo_ref, fhi_ref,
                     dwp_ref, own_ref, low_ref, high_ref, ext, dext, dw, total, grad):
    ext[0:NB] = feat_ref[...]
    ext[NB : NB + KB] = elow_ref[0]
    ext[NB + KB :] = ehigh_ref[0]
    total[...] = hown_ref[...]
    for j in range(KB):
        total[slo_ref[0, j]] += flo_ref[j].astype(F32)
        total[shi_ref[0, j]] += fhi_ref[j].astype(F32)
    grad[...] = jnp.where(pre_ref[...] > 0, total[...], 0.0).astype(BF16)
    layer_body(count_ref, pin_ref, poff_ref, rmap_ref, w_ref, ext, grad, dwp_ref, own_ref, low_ref, high_ref, dext, dw)


LAYER_OUT = (
    jax.ShapeDtypeStruct((PACKED, ROW), F32),
    jax.ShapeDtypeStruct((NB, C, ROW), F32),
    jax.ShapeDtypeStruct((KB, C, ROW), BF16),
    jax.ShapeDtypeStruct((KB, C, ROW), BF16),
)
LAYER_SCRATCH = [
    pltpu.VMEM((EXT, C, ROW), BF16),
    pltpu.VMEM((EXT, C, ROW), F32),
    pltpu.VMEM((K + 1, C, ROW), F32),
]


def layer_two(count, pin, poff, rmap, w, pre_act, low, high, out_grad):
    return pl.pallas_call(
        layer_two_kernel,
        out_shape=LAYER_OUT,
        in_specs=[SMEM] * 3 + [VMEM] * 6,
        out_specs=(VMEM,) * 4,
        scratch_shapes=LAYER_SCRATCH,
        compiler_params=pltpu.CompilerParams(vmem_limit_bytes=VMEM_LIMIT),
        name="layer_two",
    )(count, pin, poff, rmap, w, pre_act, low, high, out_grad)


def layer_one(count, pin, poff, rmap, w, features, low, high, slo, shi, pre_act, hown, flo, fhi):
    return pl.pallas_call(
        layer_one_kernel,
        out_shape=LAYER_OUT,
        in_specs=[SMEM] * 3 + [VMEM] * 5 + [SMEM] * 2 + [VMEM] * 4,
        out_specs=(VMEM,) * 4,
        scratch_shapes=LAYER_SCRATCH + [pltpu.VMEM((NB, C, ROW), F32), pltpu.VMEM((NB, C, ROW), BF16)],
        compiler_params=pltpu.CompilerParams(vmem_limit_bytes=VMEM_LIMIT),
        name="layer_one",
    )(count, pin, poff, rmap, w, features, low, high, slo, shi, pre_act, hown, flo, fhi)


def reduce_kernel(ny, nz, nx, dw1_ref, dw2_ref, low_ref, high_ref, g1_ref, g2_ref, lo_ref, hi_ref,
                  in_lo, in_hi, snd0, rcv0, acc1, snd1, rcv1, acc2, snd2, rcv2, gat3, fin2, fin1,
                  sb, rb, s0, r0, s1, r1, s2, r2, s3, r3, s4, r4, s5, r5, s6, r6):
    half = PACKED // 2
    district = lax.axis_index("district")
    tile = lax.axis_index("tile")
    core = lax.rem(district, 2)
    y = lax.div(district, 2)
    z = lax.div(tile, nx)
    x = lax.rem(tile, nx)
    below, above, has_below, has_above = tile_neighbours()
    other = (district + 1 - 2 * core, tile)
    ys = [lax.rem(y + s, ny) for s in range(1, ny)]
    zs = [lax.rem(z + s, nz) for s in range(1, nz)]
    y_peers = [(i * 2 + core, tile) for i in ys]
    z_peers = [(district, i * nx + x) for i in zs]
    x_peers = [(district, z * nx + lax.rem(x + s, nx)) for s in range(1, nx)]
    along_y = (ny, y, ys, y_peers)
    along_z = (nz, z, zs, z_peers)
    first = (along_y, along_z)
    second = (along_z, along_y)
    outs = (g1_ref, g2_ref)
    dws = (dw1_ref, dw2_ref)

    greet([below, above, other] + y_peers + z_peers + x_peers)

    up = remote(high_ref, in_lo, sb.at[0], rb.at[0], above)
    down = remote(low_ref, in_hi, sb.at[1], rb.at[1], below)

    keep = pl.ds(pl.multiple_of(core * half, half), half)
    away = pl.ds(pl.multiple_of((1 - core) * half, half), half)
    swaps = []
    for g in range(2):
        snd0[g] = dws[g][away, :].astype(BF16)
        swaps.append(remote(snd0.at[g], rcv0.at[g], s0.at[g], r0.at[g], other))
        swaps[g].start()
    up.start()
    down.start()

    stage1 = [[], []]
    for g in range(2):
        n, me, others, peers = first[g]
        part = half // n
        swaps[g].wait()
        acc1[g] = dws[g][keep, :] + rcv0[g].astype(F32)
        snd1[g] = acc1[g].astype(BF16)
        for s in range(n - 1):
            rows = pl.ds(pl.multiple_of(others[s] * part, part), part)
            copy = remote(snd1.at[g, rows, :], rcv1.at[g, s], s1.at[g, s], r1.at[g, s], peers[s])
            copy.start()
            stage1[g].append(copy)

    stage2 = [[], []]
    for g in range(2):
        n, me, others, peers = first[g]
        part = half // n
        total = acc1[g, pl.ds(pl.multiple_of(me * part, part), part), :]
        for s in range(n - 1):
            stage1[g][s].wait()
            total = total + rcv1[g, s].astype(F32)
        acc2[g] = total
        snd2[g] = total.astype(BF16)
        n, me, others, peers = second[g]
        part = part // n
        for s in range(n - 1):
            rows = pl.ds(pl.multiple_of(others[s] * part, part), part)
            copy = remote(snd2.at[g, rows, :], rcv2.at[g, s], s2.at[g, s], r2.at[g, s], peers[s])
            copy.start()
            stage2[g].append(copy)

    stage3 = [[], []]
    for g in range(2):
        n, me, others, peers = second[g]
        part = half // (ny * nz)
        total = acc2[g, pl.ds(pl.multiple_of(me * part, part), part), :]
        for s in range(n - 1):
            stage2[g][s].wait()
            total = total + rcv2[g, s].astype(F32)
        gat3[g, x] = total.astype(BF16)
        for s in range(nx - 1):
            copy = remote(gat3.at[g, x], gat3.at[g, x], s3.at[g, s], r3.at[g, s], x_peers[s])
            copy.start()
            stage3[g].append(copy)

    stage4 = [[], []]
    for g in range(2):
        n, me, others, peers = second[g]
        part = half // (ny * nz)
        for copy in stage3[g]:
            copy.wait()
        total = gat3[g, 0].astype(F32)
        for i in range(1, nx):
            total = total + gat3[g, i].astype(F32)
        rows = pl.ds(pl.multiple_of(me * part, part), part)
        fin2[g, rows, :] = total.astype(BF16)
        for s in range(n - 1):
            copy = remote(fin2.at[g, rows, :], fin2.at[g, rows, :], s4.at[g, s], r4.at[g, s], peers[s])
            copy.start()
            stage4[g].append(copy)

    stage5 = [[], []]
    for g in range(2):
        n, me, others, peers = first[g]
        part = half // n
        for copy in stage4[g]:
            copy.wait()
        rows = pl.ds(pl.multiple_of(me * part, part), part)
        fin1[g, rows, :] = fin2[g]
        for s in range(n - 1):
            copy = remote(fin2.at[g], fin1.at[g, rows, :], s5.at[g, s], r5.at[g, s], peers[s])
            copy.start()
            stage5[g].append(copy)

    up.wait()
    lo_ref[...] = jnp.where(has_below, in_lo[...], jnp.zeros_like(in_lo))
    down.wait()
    hi_ref[...] = jnp.where(has_above, in_hi[...], jnp.zeros_like(in_hi))

    stage6 = []
    for g in range(2):
        for copy in stage5[g]:
            copy.wait()
        copy = remote(fin1.at[g], outs[g].at[keep, :], s6.at[g], r6.at[g], other)
        copy.start()
        stage6.append(copy)
        outs[g][keep, :] = fin1[g]
    for copy in stage6:
        copy.wait()


def reduce_all(ny, nz, nx, dw1, dw2, low, high):
    half = PACKED // 2
    most = max(ny, nz)
    least = min(ny, nz)
    packed = jax.ShapeDtypeStruct((PACKED, ROW), BF16)
    part = jax.ShapeDtypeStruct((KB, C, ROW), BF16)
    last = half // (ny * nz)
    dma = pltpu.SemaphoreType.DMA
    return pl.pallas_call(
        functools.partial(reduce_kernel, ny, nz, nx),
        out_shape=(packed, packed, part, part),
        in_specs=[VMEM] * 4,
        out_specs=(VMEM,) * 4,
        scratch_shapes=[
            pltpu.VMEM((KB, C, ROW), BF16),
            pltpu.VMEM((KB, C, ROW), BF16),
            pltpu.VMEM((2, half, ROW), BF16),
            pltpu.VMEM((2, half, ROW), BF16),
            pltpu.VMEM((2, half, ROW), F32),
            pltpu.VMEM((2, half, ROW), BF16),
            pltpu.VMEM((2, most - 1, half // least, ROW), BF16),
            pltpu.VMEM((2, half // least, ROW), F32),
            pltpu.VMEM((2, half // least, ROW), BF16),
            pltpu.VMEM((2, most - 1, last, ROW), BF16),
            pltpu.VMEM((2, nx, last, ROW), BF16),
            pltpu.VMEM((2, half // least, ROW), BF16),
            pltpu.VMEM((2, half, ROW), BF16),
            dma((2,)), dma((2,)),
            dma((2,)), dma((2,)),
            dma((2, most - 1)), dma((2, most - 1)),
            dma((2, most - 1)), dma((2, most - 1)),
            dma((2, nx - 1)), dma((2, nx - 1)),
            dma((2, most - 1)), dma((2, most - 1)),
            dma((2, most - 1)), dma((2, most - 1)),
            dma((2,)), dma((2,)),
        ],
        compiler_params=pltpu.CompilerParams(
            collective_id=2, has_side_effects=True, vmem_limit_bytes=VMEM_LIMIT
        ),
        name="reduce_all",
    )(dw1, dw2, low, high)


def finish_kernel(slo_ref, shi_ref, own_ref, flo_ref, fhi_ref, g1_ref, g2_ref, fg_ref, w1_ref, w2_ref, total):
    total[...] = own_ref[...]
    for j in range(KB):
        total[slo_ref[0, j]] += flo_ref[j].astype(F32)
        total[shi_ref[0, j]] += fhi_ref[j].astype(F32)
    fg_ref[...] = total[...].astype(BF16)
    lane = lax.broadcasted_iota(jnp.int32, (C, ROW), 1)
    for src, dst in ((g1_ref, w1_ref), (g2_ref, w2_ref)):
        for q in range(7):
            base = q * 3 * C
            r1 = src[base : base + C, :].astype(F32)
            r2 = src[base + C : base + 2 * C, :].astype(F32)
            r3 = src[base + 2 * C : base + 3 * C, :].astype(F32)
            dst[4 * q] = r1[:, 0:C]
            dst[4 * q + 1] = pltpu.roll(jnp.where(lane < 96, r2, r1), 32, 1)[:, 0:C]
            dst[4 * q + 2] = pltpu.roll(jnp.where(lane < 64, r3, r2), 64, 1)[:, 0:C]
            if 4 * q + 3 < K:
                dst[4 * q + 3] = pltpu.roll(r3, 96, 1)[:, 0:C]


def finish(slo, shi, own, flo, fhi, g1, g2):
    kern = jax.ShapeDtypeStruct((K, C, C), F32)
    return pl.pallas_call(
        finish_kernel,
        out_shape=(jax.ShapeDtypeStruct((NB, C, ROW), BF16), kern, kern),
        in_specs=[SMEM] * 2 + [VMEM] * 5,
        out_specs=(VMEM,) * 3,
        scratch_shapes=[pltpu.VMEM((NB, C, ROW), F32)],
        compiler_params=pltpu.CompilerParams(vmem_limit_bytes=VMEM_LIMIT),
        name="finish",
    )(slo, shi, own, flo, fhi, g1, g2)


def body(ny, nz, nx, features, pre_act, out_grad, weight_one, weight_two, block_count, pair_in, pair_off,
         row_map, send_lo, send_hi):
    low, high = halo(send_lo, send_hi, features, pre_act)
    dw2, hown, hlow, hhigh = layer_two(
        block_count, pair_in, pair_off, row_map, weight_two, pre_act, low, high, out_grad
    )
    flo, fhi = give_back(hlow, hhigh)
    dw1, own, dlow, dhigh = layer_one(
        block_count, pair_in, pair_off, row_map, weight_one, features, low, high,
        send_lo, send_hi, pre_act, hown, flo, fhi,
    )
    g1, g2, xlo, xhi = reduce_all(ny, nz, nx, dw1, dw2, dlow, dhigh)
    return finish(send_lo, send_hi, own, xlo, xhi, g1, g2)


def solution(mesh):
    placed = (
        P(("district", "tile"), None, None),
        P(("district", "tile"), None, None),
        P(("district", "tile"), None, None),
        P(),
        P(),
        P(("district", "tile")),
        P(("district", "tile"), None),
        P(("district", "tile"), None),
        P(("district", "tile"), None, None),
        P(("district", "tile"), None),
        P(("district", "tile"), None),
    )
    tiles = mesh.shape["tile"]
    nx = 4 if tiles % 4 == 0 and tiles > 4 else 2
    ny, nz = mesh.shape["district"] // 2, tiles // nx
    return jax.shard_map(
        functools.partial(body, ny, nz, nx),
        mesh=mesh,
        in_specs=placed,
        out_specs=(P(("district", "tile"), None, None), P(), P()),
        check_vma=False,
    )
```

```python
import functools

import jax
import jax.numpy as jnp
from jax import lax
from jax.experimental import pallas as pl
from jax.experimental.pallas import tpu as pltpu
from jax.sharding import PartitionSpec as P

K = 27
PB = 16
NB = 4
KB = 4
C = 96
ROW = 128
EXT = NB + 2 * KB
PAIRS = NB * PB
UNROLL = 32
NT = (((1,), (1,)), ((), ()))
PACKED = 2048
F32 = jnp.float32
BF16 = jnp.bfloat16
VMEM_LIMIT = 56 * 1024 * 1024

HBM = pl.BlockSpec(memory_space=pltpu.HBM)
SMEM = pl.BlockSpec(memory_space=pltpu.SMEM)
VMEM = pl.BlockSpec(memory_space=pltpu.VMEM)


def remote(src, dst, send_sem, recv_sem, where):
    return pltpu.make_async_remote_copy(
        src_ref=src,
        dst_ref=dst,
        send_sem=send_sem,
        recv_sem=recv_sem,
        device_id=where,
        device_id_type=pl.DeviceIdType.MESH,
    )


def tile_neighbours():
    district = lax.axis_index("district")
    tile = lax.axis_index("tile")
    tiles = lax.axis_size("tile")
    below = (district, lax.rem(tile + tiles - 1, tiles))
    above = (district, lax.rem(tile + 1, tiles))
    has_below = tile > 0
    has_above = tile < tiles - 1
    return below, above, has_below, has_above


def sort_pairs(keys, table, row):
    p = lax.broadcasted_iota(jnp.int32, (PAIRS, PAIRS), 0)
    q = lax.broadcasted_iota(jnp.int32, (PAIRS, PAIRS), 1)
    column = jnp.sum(jnp.where(p == q, keys, 0), axis=1, keepdims=True)
    ahead = jnp.logical_or(keys < column, jnp.logical_and(keys == column, q < p))
    rank = jnp.sum(jnp.where(ahead, 1, 0), axis=1, keepdims=True)
    table[row : row + 1, 0:PAIRS] = jnp.sum(jnp.where(rank == q, p, 0), axis=0, keepdims=True)
    lane = lax.broadcasted_iota(jnp.int32, (PAIRS, ROW), 1)
    table[row + 1 : row + 2, :] = jnp.sum(jnp.where(column <= lane, 1, 0), axis=0, keepdims=True)
    table[row + 2 : row + 3, :] = jnp.sum(jnp.where(column < lane, 1, 0), axis=0, keepdims=True)


def build_picks(rmap, count, picks):
    rows = lax.broadcasted_iota(jnp.int32, (ROW, ROW), 0)

    def block(o, carry):
        maps = rmap[0, pl.ds(pl.multiple_of(o * PB, PB), PB), :] + jnp.where(o < count, 0, 2 * ROW)
        for j in range(PB):
            picks[o * PB + j] = jnp.where(rows == maps[j : j + 1, :], 1.0, 0.0).astype(BF16)
        return carry

    lax.fori_loop(0, NB, block, 0)


def scatter_grads(picks, gt, ht):
    def step(i, carry):
        for j in range(UNROLL):
            product = jnp.dot(picks[i * UNROLL + j], gt[i * (UNROLL // PB) + j // PB], preferred_element_type=F32)
            ht[i * UNROLL + j] = product.astype(BF16)
        return carry

    lax.fori_loop(0, PAIRS // UNROLL, step, 0)


def running_sums(product, row, keys, table, sums):
    def step(i, carry):
        total, before = carry
        for j in range(UNROLL):
            at = i * UNROLL + j
            p = table[row, at]
            key = keys[0, p]
            total = total * jnp.where(key == before, 1.0, 0.0) + product(p)
            sums[at] = total
            before = key
        return total, before

    lax.fori_loop(0, PAIRS // UNROLL, step, (jnp.zeros((C, ROW), F32), jnp.int32(-1)))


def sum_of(key, row, table, sums):
    upto = table[row + 1, key]
    some = jnp.where(upto > table[row + 2, key], 1.0, 0.0)
    return sums[jnp.maximum(upto - 1, 0)] * some


def pack(table, sums, packed):
    lane = lax.broadcasted_iota(jnp.int32, (C, ROW), 1)

    def group(q, carry):
        a = sum_of(4 * q, 0, table, sums)
        b = pltpu.roll(sum_of(4 * q + 1, 0, table, sums), 96, 1)
        c = pltpu.roll(sum_of(4 * q + 2, 0, table, sums), 64, 1)
        d = pltpu.roll(sum_of(4 * q + 3, 0, table, sums), 32, 1)
        base = pl.multiple_of(q * 3 * C, 3 * C)
        packed[pl.ds(base, C), :] = jnp.where(lane < 96, a, b)
        packed[pl.ds(base + C, C), :] = jnp.where(lane < 64, b, c)
        packed[pl.ds(base + 2 * C, C), :] = jnp.where(lane < 32, c, d)
        return carry

    lax.fori_loop(0, 7, group, 0)
    packed[21 * C :, :] = jnp.zeros((PACKED - 21 * C, ROW), F32)


def fused_kernel(ny, nz, nx, *refs):
    (feat_in, pre_in, og_in, w1_in, w2_in, count_in, pin_in, poff_in, rmap_in, slo_in, shi_in,
     g1_ref, g2_ref, own_ref, xlo_ref, xhi_ref,
     feat, pre, og, w1, w2, rmap, pin_v, poff_v, count, pin, poff, slo, shi, table_v, table,
     picks, gt, ht, sums, ext_h, ext_x, own2,
     out_lo, out_hi, in_lo, in_hi, gb_lo, gb_hi, fb_lo, fb_hi, gb2_lo, gb2_hi,
     dwp, rcv0, snd1, rcv1, mine, gat3, fin1,
     load, tsem, hs, hr, gs, gr, g2s, g2r, s0, r0, s1, r1, s3, r3, s5, r5, s6, r6) = refs
    half = PACKED // 2
    part = half // (ny * nx)
    district = lax.axis_index("district")
    tile = lax.axis_index("tile")
    core = lax.rem(district, 2)
    y = lax.div(district, 2)
    z = lax.div(tile, nx)
    x = lax.rem(tile, nx)
    below, above, has_below, has_above = tile_neighbours()
    other = (district + 1 - 2 * core, tile)

    def reach(step):
        return -min(step[0], ny - step[0]) - min(step[1], nx - step[1])

    steps = sorted([(a, b) for a in range(ny) for b in range(nx) if a + b], key=reach)
    plane = [(lax.rem(y + a, ny), lax.rem(x + b, nx)) for a, b in steps]
    plane_peers = [(i * 2 + core, z * nx + j) for i, j in plane]
    z_order = sorted(range(1, nz), key=lambda a: -min(a, nz - a))
    z_peers = [(district, lax.rem(z + a, nz) * nx + x) for a in z_order]

    loads = {}
    pieces = (("rmap", rmap_in, rmap), ("count", count_in, count), ("poff_v", poff_in, poff_v), ("pin_v", pin_in, pin_v),
              ("og", og_in, og), ("pin", pin_in, pin), ("poff", poff_in, poff), ("slo", slo_in, slo), ("shi", shi_in, shi),
              ("pre", pre_in, pre), ("feat", feat_in, feat), ("w2", w2_in, w2), ("w1", w1_in, w1))
    for i, (name, src, dst) in enumerate(pieces):
        loads[name] = pltpu.make_async_copy(src, dst, load.at[i])
        loads[name].start()
    barrier = pltpu.get_barrier_semaphore()
    peers = plane_peers + z_peers + [other, below, above]
    for peer in peers:
        pl.semaphore_signal(barrier, inc=1, device_id=peer, device_id_type=pl.DeviceIdType.MESH)

    gt[...] = jnp.zeros_like(gt)
    table_v[...] = jnp.zeros_like(table_v)
    loads["poff_v"].wait()
    loads["pin_v"].wait()
    sort_pairs(poff_v[...], table_v, 0)
    sort_pairs(pin_v[...], table_v, 3)
    to_scalar = pltpu.make_async_copy(table_v, table, tsem)
    to_scalar.start()
    loads["rmap"].wait()
    loads["count"].wait()
    build_picks(rmap, count[0], picks)
    loads["og"].wait()
    for b in range(NB):
        gt[b, :, 0:C] = jnp.transpose(og[b])
    scatter_grads(picks, gt, ht)

    for name in ("slo", "shi", "pre", "feat"):
        loads[name].wait()
    for j in range(KB):
        out_lo[0, j] = jnp.maximum(pre[slo[0, j]], 0.0)
        out_hi[0, j] = jnp.maximum(pre[shi[0, j]], 0.0)
        out_lo[1, j] = feat[slo[0, j]]
        out_hi[1, j] = feat[shi[0, j]]
    pl.semaphore_wait(barrier, len(peers))
    halo = []
    for f in range(2):
        halo.append((
            remote(out_hi.at[f], in_lo.at[f], hs.at[0, f], hr.at[0, f], above),
            remote(out_lo.at[f], in_hi.at[f], hs.at[1, f], hr.at[1, f], below),
        ))
    for copy in halo[0]:
        copy.start()

    for name in ("pin", "poff", "w2"):
        loads[name].wait()
    to_scalar.wait()
    running_sums(
        lambda p: lax.dot_general(w2[poff[0, p]], ht[p, :, 0:C], NT, preferred_element_type=F32),
        3, pin, table, sums,
    )
    for j in range(KB):
        gb_lo[j] = sum_of(NB + j, 3, table, sums).astype(gb_lo.dtype)
        gb_hi[j] = sum_of(NB + KB + j, 3, table, sums).astype(gb_hi.dtype)
    back = (
        remote(gb_hi, fb_lo, gs.at[0], gr.at[0], above),
        remote(gb_lo, fb_hi, gs.at[1], gr.at[1], below),
    )
    for copy in back:
        copy.start()
    for copy in halo[1]:
        copy.start()
    for b in range(NB):
        own2[b] = sum_of(b, 3, table, sums)

    def extend(f, own, ext):
        ext[0:NB] = own
        halo[f][0].wait()
        ext[NB : NB + KB] = jnp.where(has_below, in_lo[f], jnp.zeros_like(in_lo[f]))
        halo[f][1].wait()
        ext[NB + KB :] = jnp.where(has_above, in_hi[f], jnp.zeros_like(in_hi[f]))

    def weight_sums(ext):
        running_sums(
            lambda p: jnp.dot(ext[pin[0, p]], ht[p], preferred_element_type=F32), 0, poff, table, sums
        )

    keep = pl.ds(pl.multiple_of(core * half, half), half)
    away = pl.ds(pl.multiple_of((1 - core) * half, half), half)
    chunk = pl.ds(pl.multiple_of((y * nx + x) * part, part), part)
    outs = (g1_ref, g2_ref)

    def swap_halves(g):
        copy = remote(dwp.at[g, away, :], rcv0.at[g], s0.at[g], r0.at[g], other)
        copy.start()
        return [copy]

    def scatter_plane(g, waits):
        for copy in waits:
            copy.wait()
        snd1[g] = (dwp[g, keep, :] + rcv0[g]).astype(BF16)
        copies = []
        for s in range(len(plane)):
            i, j = plane[s]
            rows = pl.ds(pl.multiple_of((i * nx + j) * part, part), part)
            copies.append(remote(snd1.at[g, rows, :], rcv1.at[g, s], s1.at[g, s], r1.at[g, s], plane_peers[s]))
            copies[s].start()
        at = pl.ds(pl.multiple_of(core * half + (y * nx + x) * part, part), part)
        mine[g] = dwp[g, at, :] + rcv0[g, chunk, :]
        return copies

    def exchange_z(g, waits):
        for copy in waits:
            copy.wait()
        total = mine[g]
        for s in range(len(plane)):
            total = total + rcv1[g, s].astype(F32)
        gat3[g, z] = total.astype(BF16)
        copies = []
        for s in range(nz - 1):
            copies.append(remote(gat3.at[g, z], gat3.at[g, z], s3.at[g, s], r3.at[g, s], z_peers[s]))
            copies[s].start()
        return copies

    def gather_plane(g, waits):
        for copy in waits:
            copy.wait()
        total = gat3[g, 0].astype(F32)
        for i in range(1, nz):
            total = total + gat3[g, i].astype(F32)
        fin1[g, chunk, :] = total.astype(BF16)
        copies = []
        for s in range(len(plane)):
            copies.append(remote(fin1.at[g, chunk, :], fin1.at[g, chunk, :], s5.at[g, s], r5.at[g, s], plane_peers[s]))
            copies[s].start()
        return copies

    def share_halves(g, waits):
        for copy in waits:
            copy.wait()
        copy = remote(fin1.at[g], outs[g].at[keep, :], s6.at[g], r6.at[g], other)
        copy.start()
        outs[g][keep, :] = fin1[g]
        return [copy]

    extend(0, jnp.maximum(pre[...], 0.0), ext_h)
    weight_sums(ext_h)
    pack(table, sums, dwp.at[1])
    two = swap_halves(1)
    two = scatter_plane(1, two)

    for copy in back:
        copy.wait()
    for b in range(NB):
        total = own2[b]
        for j in range(KB):
            from_below = jnp.where(jnp.logical_and(slo[0, j] == b, has_below), 1.0, 0.0)
            from_above = jnp.where(jnp.logical_and(shi[0, j] == b, has_above), 1.0, 0.0)
            total = total + from_below * fb_lo[j].astype(F32) + from_above * fb_hi[j].astype(F32)
        gt[b, :, 0:C] = jnp.transpose(jnp.where(pre[b] > 0, total, 0.0).astype(BF16))
    scatter_grads(picks, gt, ht)
    extend(1, feat[...], ext_x)
    weight_sums(ext_x)
    pack(table, sums, dwp.at[0])
    one = swap_halves(0)
    two = exchange_z(1, two)
    one = scatter_plane(0, one)

    loads["w1"].wait()
    running_sums(
        lambda p: lax.dot_general(w1[poff[0, p]], ht[p, :, 0:C], NT, preferred_element_type=F32),
        3, pin, table, sums,
    )
    for j in range(KB):
        gb2_lo[j] = sum_of(NB + j, 3, table, sums)
        gb2_hi[j] = sum_of(NB + KB + j, 3, table, sums)
    for b in range(NB):
        own_ref[b] = sum_of(b, 3, table, sums)

    one = exchange_z(0, one)
    last = (
        remote(gb2_hi, xlo_ref, g2s.at[0], g2r.at[0], above),
        remote(gb2_lo, xhi_ref, g2s.at[1], g2r.at[1], below),
    )
    for copy in last:
        copy.start()
    two = gather_plane(1, two)
    one = gather_plane(0, one)
    two = share_halves(1, two)
    one = share_halves(0, one)
    for copy in list(last) + two + one:
        copy.wait()


def fused(ny, nz, nx, *operands):
    half = PACKED // 2
    part = half // (ny * nx)
    near = ny * nx - 1
    dma = pltpu.SemaphoreType.DMA
    packed = jax.ShapeDtypeStruct((PACKED, ROW), BF16)
    blocks = jax.ShapeDtypeStruct((NB, C, ROW), F32)
    four = pltpu.VMEM((NB, C, ROW), BF16)
    four_wide = pltpu.VMEM((NB, C, ROW), F32)
    kernel_weights = pltpu.VMEM((K, C, C), BF16)
    return pl.pallas_call(
        functools.partial(fused_kernel, ny, nz, nx),
        out_shape=(packed, packed, blocks, blocks, blocks),
        in_specs=[HBM] * 11,
        out_specs=(VMEM,) * 5,
        scratch_shapes=[
            four, four, four, kernel_weights, kernel_weights,
            pltpu.VMEM((1, PAIRS, ROW), jnp.int32),
            pltpu.VMEM((1, PAIRS), jnp.int32),
            pltpu.VMEM((1, PAIRS), jnp.int32),
            pltpu.SMEM((1,), jnp.int32),
            pltpu.SMEM((1, PAIRS), jnp.int32),
            pltpu.SMEM((1, PAIRS), jnp.int32),
            pltpu.SMEM((1, KB), jnp.int32),
            pltpu.SMEM((1, KB), jnp.int32),
            pltpu.VMEM((8, ROW), jnp.int32),
            pltpu.SMEM((8, ROW), jnp.int32),
            pltpu.VMEM((PAIRS, ROW, ROW), BF16),
            pltpu.VMEM((NB, ROW, ROW), BF16),
            pltpu.VMEM((PAIRS, ROW, ROW), BF16),
            pltpu.VMEM((PAIRS, C, ROW), F32),
            pltpu.VMEM((EXT, C, ROW), BF16),
            pltpu.VMEM((EXT, C, ROW), BF16),
            four_wide,
            pltpu.VMEM((2, KB, C, ROW), BF16),
            pltpu.VMEM((2, KB, C, ROW), BF16),
            pltpu.VMEM((2, KB, C, ROW), BF16),
            pltpu.VMEM((2, KB, C, ROW), BF16),
            four, four, four, four, four_wide, four_wide,
            pltpu.VMEM((2, PACKED, ROW), F32),
            pltpu.VMEM((2, half, ROW), F32),
            pltpu.VMEM((2, half, ROW), BF16),
            pltpu.VMEM((2, near, part, ROW), BF16),
            pltpu.VMEM((2, part, ROW), F32),
            pltpu.VMEM((2, nz, part, ROW), BF16),
            pltpu.VMEM((2, half, ROW), BF16),
            dma((13,)), dma,
            dma((2, 2)), dma((2, 2)),
            dma((2,)), dma((2,)),
            dma((2,)), dma((2,)),
            dma((2,)), dma((2,)),
            dma((2, near)), dma((2, near)),
            dma((2, nz - 1)), dma((2, nz - 1)),
            dma((2, near)), dma((2, near)),
            dma((2,)), dma((2,)),
        ],
        compiler_params=pltpu.CompilerParams(
            collective_id=0, has_side_effects=True, vmem_limit_bytes=VMEM_LIMIT
        ),
        name="fused",
    )(*operands)


def finish_kernel(slo_ref, shi_ref, own_ref, flo_ref, fhi_ref, g1_ref, g2_ref, fg_ref, w1_ref, w2_ref, total):
    below, above, has_below, has_above = tile_neighbours()
    total[...] = own_ref[...]
    for j in range(KB):
        total[slo_ref[0, j]] += flo_ref[j] * jnp.where(has_below, 1.0, 0.0)
        total[shi_ref[0, j]] += fhi_ref[j] * jnp.where(has_above, 1.0, 0.0)
    fg_ref[...] = total[...].astype(BF16)
    lane = lax.broadcasted_iota(jnp.int32, (C, ROW), 1)
    for src, dst in ((g1_ref, w1_ref), (g2_ref, w2_ref)):
        for q in range(7):
            base = q * 3 * C
            r1 = src[base : base + C, :].astype(F32)
            r2 = src[base + C : base + 2 * C, :].astype(F32)
            r3 = src[base + 2 * C : base + 3 * C, :].astype(F32)
            dst[4 * q] = r1[:, 0:C]
            dst[4 * q + 1] = pltpu.roll(jnp.where(lane < 96, r2, r1), 32, 1)[:, 0:C]
            dst[4 * q + 2] = pltpu.roll(jnp.where(lane < 64, r3, r2), 64, 1)[:, 0:C]
            if 4 * q + 3 < K:
                dst[4 * q + 3] = pltpu.roll(r3, 96, 1)[:, 0:C]


def finish(slo, shi, own, flo, fhi, g1, g2):
    kern = jax.ShapeDtypeStruct((K, C, C), F32)
    return pl.pallas_call(
        finish_kernel,
        out_shape=(jax.ShapeDtypeStruct((NB, C, ROW), BF16), kern, kern),
        in_specs=[SMEM] * 2 + [VMEM] * 5,
        out_specs=(VMEM,) * 3,
        scratch_shapes=[pltpu.VMEM((NB, C, ROW), F32)],
        compiler_params=pltpu.CompilerParams(vmem_limit_bytes=VMEM_LIMIT),
        name="finish",
    )(slo, shi, own, flo, fhi, g1, g2)


def body(ny, nz, nx, features, pre_act, out_grad, weight_one, weight_two, block_count, pair_in, pair_off,
         row_map, send_lo, send_hi):
    g1, g2, own, xlo, xhi = fused(
        ny, nz, nx, features, pre_act, out_grad, weight_one, weight_two, block_count, pair_in, pair_off,
        row_map, send_lo, send_hi,
    )
    return finish(send_lo, send_hi, own, xlo, xhi, g1, g2)


def solution(mesh):
    placed = (
        P(("district", "tile"), None, None),
        P(("district", "tile"), None, None),
        P(("district", "tile"), None, None),
        P(),
        P(),
        P(("district", "tile")),
        P(("district", "tile"), None),
        P(("district", "tile"), None),
        P(("district", "tile"), None, None),
        P(("district", "tile"), None),
        P(("district", "tile"), None),
    )
    tiles = mesh.shape["tile"]
    nx = 4 if tiles % 4 == 0 and tiles > 4 else 2
    ny, nz = mesh.shape["district"] // 2, tiles // nx
    return jax.shard_map(
        functools.partial(body, ny, nz, nx),
        mesh=mesh,
        in_specs=placed,
        out_specs=(P(("district", "tile"), None, None), P(), P()),
        check_vma=False,
    )
```

```python
import functools

import jax
import jax.numpy as jnp
from jax import lax
from jax.experimental import pallas as pl
from jax.experimental.pallas import tpu as pltpu
from jax.sharding import PartitionSpec as P

K = 27
PB = 16
NB = 4
KB = 4
C = 96
ROW = 128
EXT = NB + 2 * KB
PAIRS = NB * PB
UNROLL = 32
NT = (((1,), (1,)), ((), ()))
PACKED = 2048
F32 = jnp.float32
BF16 = jnp.bfloat16
VMEM_LIMIT = 24 * 1024 * 1024

HBM = pl.BlockSpec(memory_space=pltpu.HBM)
SMEM = pl.BlockSpec(memory_space=pltpu.SMEM)
VMEM = pl.BlockSpec(memory_space=pltpu.VMEM)


def remote(src, dst, send_sem, recv_sem, where):
    return pltpu.make_async_remote_copy(
        src_ref=src,
        dst_ref=dst,
        send_sem=send_sem,
        recv_sem=recv_sem,
        device_id=where,
        device_id_type=pl.DeviceIdType.MESH,
    )


def tile_neighbours():
    district = lax.axis_index("district")
    tile = lax.axis_index("tile")
    tiles = lax.axis_size("tile")
    below = (district, lax.rem(tile + tiles - 1, tiles))
    above = (district, lax.rem(tile + 1, tiles))
    has_below = tile > 0
    has_above = tile < tiles - 1
    return below, above, has_below, has_above


def sort_pairs(keys, table, row):
    p = lax.broadcasted_iota(jnp.int32, (PAIRS, PAIRS), 0)
    q = lax.broadcasted_iota(jnp.int32, (PAIRS, PAIRS), 1)
    column = jnp.sum(jnp.where(p == q, keys, 0), axis=1, keepdims=True)
    ahead = jnp.logical_or(keys < column, jnp.logical_and(keys == column, q < p))
    rank = jnp.sum(jnp.where(ahead, 1, 0), axis=1, keepdims=True)
    table[row : row + 1, 0:PAIRS] = jnp.sum(jnp.where(rank == q, p, 0), axis=0, keepdims=True)
    lane = lax.broadcasted_iota(jnp.int32, (PAIRS, ROW), 1)
    table[row + 1 : row + 2, :] = jnp.sum(jnp.where(column <= lane, 1, 0), axis=0, keepdims=True)
    table[row + 2 : row + 3, :] = jnp.sum(jnp.where(column < lane, 1, 0), axis=0, keepdims=True)


def build_picks(rmap, count, picks):
    rows = lax.broadcasted_iota(jnp.int32, (ROW, ROW), 0)

    def block(o, carry):
        maps = rmap[0, pl.ds(pl.multiple_of(o * PB, PB), PB), :] + jnp.where(o < count, 0, 2 * ROW)
        for j in range(PB):
            picks[o * PB + j] = jnp.where(rows == maps[j : j + 1, :], 1.0, 0.0).astype(BF16)
        return carry

    lax.fori_loop(0, NB, block, 0)


def scatter_grads(picks, gt, ht):
    def step(i, carry):
        for j in range(UNROLL):
            product = jnp.dot(picks[i * UNROLL + j], gt[i * (UNROLL // PB) + j // PB], preferred_element_type=F32)
            ht[i * UNROLL + j] = product.astype(BF16)
        return carry

    lax.fori_loop(0, PAIRS // UNROLL, step, 0)


def gather_rows(picks, pin, ext, gathered):
    def step(i, carry):
        for j in range(UNROLL):
            p = i * UNROLL + j
            gathered[p] = jnp.dot(ext[pin[0, p]], picks[p], preferred_element_type=F32).astype(BF16)
        return carry

    lax.fori_loop(0, PAIRS // UNROLL, step, 0)


def running_sums(product, row, keys, table, sums):
    def step(i, carry):
        total, before = carry
        for j in range(UNROLL):
            at = i * UNROLL + j
            p = table[row, at]
            key = keys[0, p]
            total = total * jnp.where(key == before, 1.0, 0.0) + product(p)
            sums[at] = total
            before = key
        return total, before

    lax.fori_loop(0, PAIRS // UNROLL, step, (jnp.zeros((C, ROW), F32), jnp.int32(-1)))


def sum_of(key, row, table, sums):
    upto = table[row + 1, key]
    some = jnp.where(upto > table[row + 2, key], 1.0, 0.0)
    return sums[jnp.maximum(upto - 1, 0)] * some


def pack(table, sums, packed):
    lane = lax.broadcasted_iota(jnp.int32, (C, ROW), 1)

    def group(q, carry):
        a = sum_of(4 * q, 0, table, sums)
        b = pltpu.roll(sum_of(4 * q + 1, 0, table, sums), 96, 1)
        c = pltpu.roll(sum_of(4 * q + 2, 0, table, sums), 64, 1)
        d = pltpu.roll(sum_of(4 * q + 3, 0, table, sums), 32, 1)
        base = pl.multiple_of(q * 3 * C, 3 * C)
        packed[pl.ds(base, C), :] = jnp.where(lane < 96, a, b)
        packed[pl.ds(base + C, C), :] = jnp.where(lane < 64, b, c)
        packed[pl.ds(base + 2 * C, C), :] = jnp.where(lane < 32, c, d)
        return carry

    lax.fori_loop(0, 7, group, 0)
    packed[21 * C :, :] = jnp.zeros((PACKED - 21 * C, ROW), F32)


def fused_kernel(ny, nz, nx, *refs):
    (feat_in, pre_in, og_in, w1_in, w2_in, count_in, pin_in, poff_in, rmap_in, slo_in, shi_in,
     g1_ref, g2_ref, own_ref, xlo_ref, xhi_ref,
     feat, pre, og, w1, w2, rmap, pin_v, poff_v, count, pin, poff, slo, shi, table_v, table,
     picks, gt, ht, gathered, sums, ext_h, ext_x, own2,
     out_lo, out_hi, in_lo, in_hi, gb_lo, gb_hi, fb_lo, fb_hi, gb2_lo, gb2_hi,
     dwp, rcv0, snd1, rcv1, mine, gat3, fin1,
     load, tsem, hs, hr, gs, gr, g2s, g2r, s0, r0, s1, r1, s3, r3, s5, r5, s6, r6) = refs
    half = PACKED // 2
    part = half // (ny * nx)
    district = lax.axis_index("district")
    tile = lax.axis_index("tile")
    core = lax.rem(district, 2)
    y = lax.div(district, 2)
    z = lax.div(tile, nx)
    x = lax.rem(tile, nx)
    below, above, has_below, has_above = tile_neighbours()
    other = (district + 1 - 2 * core, tile)

    def reach(step):
        return -min(step[0], ny - step[0]) - min(step[1], nx - step[1])

    steps = sorted([(a, b) for a in range(ny) for b in range(nx) if a + b], key=reach)
    plane = [(lax.rem(y + a, ny), lax.rem(x + b, nx)) for a, b in steps]
    plane_peers = [(i * 2 + core, z * nx + j) for i, j in plane]
    z_order = sorted(range(1, nz), key=lambda a: -min(a, nz - a))
    z_peers = [(district, lax.rem(z + a, nz) * nx + x) for a in z_order]

    loads = {}
    pieces = (("rmap", rmap_in, rmap), ("count", count_in, count), ("poff_v", poff_in, poff_v), ("pin_v", pin_in, pin_v),
              ("og", og_in, og), ("pin", pin_in, pin), ("poff", poff_in, poff), ("slo", slo_in, slo), ("shi", shi_in, shi),
              ("pre", pre_in, pre), ("feat", feat_in, feat), ("w2", w2_in, w2), ("w1", w1_in, w1))
    for i, (name, src, dst) in enumerate(pieces):
        loads[name] = pltpu.make_async_copy(src, dst, load.at[i])
        loads[name].start()
    barrier = pltpu.get_barrier_semaphore()
    peers = plane_peers + z_peers + [other, below, above]
    for peer in peers:
        pl.semaphore_signal(barrier, inc=1, device_id=peer, device_id_type=pl.DeviceIdType.MESH)

    gt[...] = jnp.zeros_like(gt)
    table_v[...] = jnp.zeros_like(table_v)
    loads["poff_v"].wait()
    loads["pin_v"].wait()
    sort_pairs(poff_v[...], table_v, 0)
    sort_pairs(pin_v[...], table_v, 3)
    to_scalar = pltpu.make_async_copy(table_v, table, tsem)
    to_scalar.start()
    loads["rmap"].wait()
    loads["count"].wait()
    build_picks(rmap, count[0], picks)
    loads["og"].wait()
    for b in range(NB):
        gt[b, :, 0:C] = jnp.transpose(og[b])
    scatter_grads(picks, gt, ht)

    for name in ("slo", "shi", "pre", "feat"):
        loads[name].wait()
    for j in range(KB):
        out_lo[0, j] = jnp.maximum(pre[slo[0, j]], 0.0)
        out_hi[0, j] = jnp.maximum(pre[shi[0, j]], 0.0)
        out_lo[1, j] = feat[slo[0, j]]
        out_hi[1, j] = feat[shi[0, j]]
    pl.semaphore_wait(barrier, len(peers))
    halo = []
    for f in range(2):
        halo.append((
            remote(out_hi.at[f], in_lo.at[f], hs.at[0, f], hr.at[0, f], above),
            remote(out_lo.at[f], in_hi.at[f], hs.at[1, f], hr.at[1, f], below),
        ))
    for copy in halo[0]:
        copy.start()

    for name in ("pin", "poff", "w2"):
        loads[name].wait()
    to_scalar.wait()
    running_sums(
        lambda p: lax.dot_general(w2[poff[0, p]], ht[p, :, 0:C], NT, preferred_element_type=F32),
        3, pin, table, sums,
    )
    for j in range(KB):
        gb_lo[j] = sum_of(NB + j, 3, table, sums).astype(gb_lo.dtype)
        gb_hi[j] = sum_of(NB + KB + j, 3, table, sums).astype(gb_hi.dtype)
    back = (
        remote(gb_hi, fb_lo, gs.at[0], gr.at[0], above),
        remote(gb_lo, fb_hi, gs.at[1], gr.at[1], below),
    )
    for copy in back:
        copy.start()
    for copy in halo[1]:
        copy.start()
    for b in range(NB):
        own2[b] = sum_of(b, 3, table, sums)

    def extend(f, own, ext):
        ext[0:NB] = own
        halo[f][0].wait()
        ext[NB : NB + KB] = jnp.where(has_below, in_lo[f], jnp.zeros_like(in_lo[f]))
        halo[f][1].wait()
        ext[NB + KB :] = jnp.where(has_above, in_hi[f], jnp.zeros_like(in_hi[f]))

    keep = pl.ds(pl.multiple_of(core * half, half), half)
    away = pl.ds(pl.multiple_of((1 - core) * half, half), half)
    chunk = pl.ds(pl.multiple_of((y * nx + x) * part, part), part)
    outs = (g1_ref, g2_ref)

    def swap_halves(g):
        copy = remote(dwp.at[g, away, :], rcv0.at[g], s0.at[g], r0.at[g], other)
        copy.start()
        return [copy]

    def scatter_plane(g, waits):
        for copy in waits:
            copy.wait()
        snd1[g] = (dwp[g, keep, :] + rcv0[g]).astype(BF16)
        copies = []
        for s in range(len(plane)):
            i, j = plane[s]
            rows = pl.ds(pl.multiple_of((i * nx + j) * part, part), part)
            copies.append(remote(snd1.at[g, rows, :], rcv1.at[g, s], s1.at[g, s], r1.at[g, s], plane_peers[s]))
            copies[s].start()
        at = pl.ds(pl.multiple_of(core * half + (y * nx + x) * part, part), part)
        mine[g] = dwp[g, at, :] + rcv0[g, chunk, :]
        return copies

    def exchange_z(g, waits):
        for copy in waits:
            copy.wait()
        total = mine[g]
        for s in range(len(plane)):
            total = total + rcv1[g, s].astype(F32)
        gat3[g, z] = total.astype(BF16)
        copies = []
        for s in range(nz - 1):
            copies.append(remote(gat3.at[g, z], gat3.at[g, z], s3.at[g, s], r3.at[g, s], z_peers[s]))
            copies[s].start()
        return copies

    def gather_plane(g, waits):
        for copy in waits:
            copy.wait()
        total = gat3[g, 0].astype(F32)
        for i in range(1, nz):
            total = total + gat3[g, i].astype(F32)
        fin1[g, chunk, :] = total.astype(BF16)
        copies = []
        for s in range(len(plane)):
            copies.append(remote(fin1.at[g, chunk, :], fin1.at[g, chunk, :], s5.at[g, s], r5.at[g, s], plane_peers[s]))
            copies[s].start()
        return copies

    def share_halves(g, waits):
        for copy in waits:
            copy.wait()
        copy = remote(fin1.at[g], outs[g].at[keep, :], s6.at[g], r6.at[g], other)
        copy.start()
        outs[g][keep, :] = fin1[g]
        return [copy]

    extend(0, jnp.maximum(pre[...], 0.0), ext_h)
    running_sums(
        lambda p: jnp.dot(ext_h[pin[0, p]], ht[p], preferred_element_type=F32), 0, poff, table, sums
    )
    pack(table, sums, dwp.at[1])
    two = swap_halves(1)
    extend(1, feat[...], ext_x)
    gather_rows(picks, pin, ext_x, gathered)
    two = scatter_plane(1, two)

    for copy in back:
        copy.wait()
    for b in range(NB):
        total = own2[b]
        for j in range(KB):
            from_below = jnp.where(jnp.logical_and(slo[0, j] == b, has_below), 1.0, 0.0)
            from_above = jnp.where(jnp.logical_and(shi[0, j] == b, has_above), 1.0, 0.0)
            total = total + from_below * fb_lo[j].astype(F32) + from_above * fb_hi[j].astype(F32)
        gt[b, :, 0:C] = jnp.transpose(jnp.where(pre[b] > 0, total, 0.0).astype(BF16))
    running_sums(
        lambda p: jnp.dot(gathered[p], gt[p // PB], preferred_element_type=F32), 0, poff, table, sums
    )
    pack(table, sums, dwp.at[0])
    one = swap_halves(0)
    scatter_grads(picks, gt, ht)
    one = scatter_plane(0, one)
    two = exchange_z(1, two)

    loads["w1"].wait()
    running_sums(
        lambda p: lax.dot_general(w1[poff[0, p]], ht[p, :, 0:C], NT, preferred_element_type=F32),
        3, pin, table, sums,
    )
    for j in range(KB):
        gb2_lo[j] = sum_of(NB + j, 3, table, sums)
        gb2_hi[j] = sum_of(NB + KB + j, 3, table, sums)
    for b in range(NB):
        own_ref[b] = sum_of(b, 3, table, sums)

    one = exchange_z(0, one)
    two = gather_plane(1, two)
    last = (
        remote(gb2_hi, xlo_ref, g2s.at[0], g2r.at[0], above),
        remote(gb2_lo, xhi_ref, g2s.at[1], g2r.at[1], below),
    )
    for copy in last:
        copy.start()
    one = gather_plane(0, one)
    two = share_halves(1, two)
    one = share_halves(0, one)
    for copy in list(last) + two + one:
        copy.wait()


def fused(ny, nz, nx, *operands):
    half = PACKED // 2
    part = half // (ny * nx)
    near = ny * nx - 1
    dma = pltpu.SemaphoreType.DMA
    packed = jax.ShapeDtypeStruct((PACKED, ROW), BF16)
    blocks = jax.ShapeDtypeStruct((NB, C, ROW), F32)
    four = pltpu.VMEM((NB, C, ROW), BF16)
    four_wide = pltpu.VMEM((NB, C, ROW), F32)
    kernel_weights = pltpu.VMEM((K, C, C), BF16)
    return pl.pallas_call(
        functools.partial(fused_kernel, ny, nz, nx),
        out_shape=(packed, packed, blocks, blocks, blocks),
        in_specs=[HBM] * 11,
        out_specs=(VMEM,) * 5,
        scratch_shapes=[
            four, four, four, kernel_weights, kernel_weights,
            pltpu.VMEM((1, PAIRS, ROW), jnp.int32),
            pltpu.VMEM((1, PAIRS), jnp.int32),
            pltpu.VMEM((1, PAIRS), jnp.int32),
            pltpu.SMEM((1,), jnp.int32),
            pltpu.SMEM((1, PAIRS), jnp.int32),
            pltpu.SMEM((1, PAIRS), jnp.int32),
            pltpu.SMEM((1, KB), jnp.int32),
            pltpu.SMEM((1, KB), jnp.int32),
            pltpu.VMEM((8, ROW), jnp.int32),
            pltpu.SMEM((8, ROW), jnp.int32),
            pltpu.VMEM((PAIRS, ROW, ROW), BF16),
            pltpu.VMEM((NB, ROW, ROW), BF16),
            pltpu.VMEM((PAIRS, ROW, ROW), BF16),
            pltpu.VMEM((PAIRS, C, ROW), BF16),
            pltpu.VMEM((PAIRS, C, ROW), F32),
            pltpu.VMEM((EXT, C, ROW), BF16),
            pltpu.VMEM((EXT, C, ROW), BF16),
            four_wide,
            pltpu.VMEM((2, KB, C, ROW), BF16),
            pltpu.VMEM((2, KB, C, ROW), BF16),
            pltpu.VMEM((2, KB, C, ROW), BF16),
            pltpu.VMEM((2, KB, C, ROW), BF16),
            four, four, four, four, four_wide, four_wide,
            pltpu.VMEM((2, PACKED, ROW), F32),
            pltpu.VMEM((2, half, ROW), F32),
            pltpu.VMEM((2, half, ROW), BF16),
            pltpu.VMEM((2, near, part, ROW), BF16),
            pltpu.VMEM((2, part, ROW), F32),
            pltpu.VMEM((2, nz, part, ROW), BF16),
            pltpu.VMEM((2, half, ROW), BF16),
            dma((13,)), dma,
            dma((2, 2)), dma((2, 2)),
            dma((2,)), dma((2,)),
            dma((2,)), dma((2,)),
            dma((2,)), dma((2,)),
            dma((2, near)), dma((2, near)),
            dma((2, nz - 1)), dma((2, nz - 1)),
            dma((2, near)), dma((2, near)),
            dma((2,)), dma((2,)),
        ],
        compiler_params=pltpu.CompilerParams(
            collective_id=0, has_side_effects=True, vmem_limit_bytes=VMEM_LIMIT
        ),
        name="fused",
    )(*operands)


def finish_kernel(slo_ref, shi_ref, own_ref, flo_ref, fhi_ref, g1_ref, g2_ref, fg_ref, w1_ref, w2_ref,
                  total, rounded, wide, sems, last):
    lane = lax.broadcasted_iota(jnp.int32, (C, ROW), 1)
    copies = []
    for g, (src, dst) in enumerate(((g1_ref, w1_ref), (g2_ref, w2_ref))):
        for q in range(7):
            base = q * 3 * C
            size = min(4, K - 4 * q)
            r1 = src[base : base + C, :].astype(F32)
            r2 = src[base + C : base + 2 * C, :].astype(F32)
            r3 = src[base + 2 * C : base + 3 * C, :].astype(F32)
            wide[g, 4 * q] = r1[:, 0:C]
            wide[g, 4 * q + 1] = pltpu.roll(jnp.where(lane < 96, r2, r1), 32, 1)[:, 0:C]
            wide[g, 4 * q + 2] = pltpu.roll(jnp.where(lane < 64, r3, r2), 64, 1)[:, 0:C]
            if size == 4:
                wide[g, 4 * q + 3] = pltpu.roll(r3, 96, 1)[:, 0:C]
            copy = pltpu.make_async_copy(
                wide.at[g, pl.ds(4 * q, size)], dst.at[pl.ds(4 * q, size)], sems.at[g, q]
            )
            copy.start()
            copies.append(copy)
    below, above, has_below, has_above = tile_neighbours()
    total[...] = own_ref[...]
    for j in range(KB):
        total[slo_ref[0, j]] += flo_ref[j] * jnp.where(has_below, 1.0, 0.0)
        total[shi_ref[0, j]] += fhi_ref[j] * jnp.where(has_above, 1.0, 0.0)
    rounded[...] = total[...].astype(BF16)
    copy = pltpu.make_async_copy(rounded, fg_ref, last)
    copy.start()
    for copy in copies + [copy]:
        copy.wait()


def finish(slo, shi, own, flo, fhi, g1, g2):
    kern = jax.ShapeDtypeStruct((K, C, C), F32)
    return pl.pallas_call(
        finish_kernel,
        out_shape=(jax.ShapeDtypeStruct((NB, C, ROW), BF16), kern, kern),
        in_specs=[SMEM] * 2 + [VMEM] * 5,
        out_specs=(HBM,) * 3,
        scratch_shapes=[
            pltpu.VMEM((NB, C, ROW), F32),
            pltpu.VMEM((NB, C, ROW), BF16),
            pltpu.VMEM((2, K, C, C), F32),
            pltpu.SemaphoreType.DMA((2, 7)),
            pltpu.SemaphoreType.DMA,
        ],
        compiler_params=pltpu.CompilerParams(vmem_limit_bytes=VMEM_LIMIT),
        name="finish",
    )(slo, shi, own, flo, fhi, g1, g2)


def body(ny, nz, nx, features, pre_act, out_grad, weight_one, weight_two, block_count, pair_in, pair_off,
         row_map, send_lo, send_hi):
    operands = (features, pre_act, out_grad, weight_one, weight_two, block_count, pair_in, pair_off,
                row_map, send_lo, send_hi)
    operands = [a if a.shape == (1,) else pltpu.with_memory_space_constraint(a, pltpu.HBM) for a in operands]
    g1, g2, own, xlo, xhi = fused(ny, nz, nx, *operands)
    return finish(send_lo, send_hi, own, xlo, xhi, g1, g2)


def solution(mesh):
    placed = (
        P(("district", "tile"), None, None),
        P(("district", "tile"), None, None),
        P(("district", "tile"), None, None),
        P(),
        P(),
        P(("district", "tile")),
        P(("district", "tile"), None),
        P(("district", "tile"), None),
        P(("district", "tile"), None, None),
        P(("district", "tile"), None),
        P(("district", "tile"), None),
    )
    tiles = mesh.shape["tile"]
    nx = 4 if tiles % 4 == 0 and tiles > 4 else 2
    ny, nz = mesh.shape["district"] // 2, tiles // nx
    return jax.shard_map(
        functools.partial(body, ny, nz, nx),
        mesh=mesh,
        in_specs=placed,
        out_specs=(P(("district", "tile"), None, None), P(), P()),
        check_vma=False,
    )
```

```python
import functools

import jax
import jax.numpy as jnp
from jax import lax
from jax.experimental import pallas as pl
from jax.experimental.pallas import tpu as pltpu
from jax.sharding import PartitionSpec as P

K = 27
PB = 16
NB = 4
KB = 4
C = 96
ROW = 128
EXT = NB + 2 * KB
PAIRS = NB * PB
UNROLL = 32
NT = (((1,), (1,)), ((), ()))
PACKED = 2048
F32 = jnp.float32
BF16 = jnp.bfloat16
VMEM_LIMIT = 24 * 1024 * 1024

HBM = pl.BlockSpec(memory_space=pltpu.HBM)
VMEM = pl.BlockSpec(memory_space=pltpu.VMEM)


def remote(src, dst, send_sem, recv_sem, where):
    return pltpu.make_async_remote_copy(
        src_ref=src,
        dst_ref=dst,
        send_sem=send_sem,
        recv_sem=recv_sem,
        device_id=where,
        device_id_type=pl.DeviceIdType.MESH,
    )


def wait_all(like, sem):
    pltpu.make_async_copy(like, like, sem).wait()


def tile_neighbours():
    district = lax.axis_index("district")
    tile = lax.axis_index("tile")
    tiles = lax.axis_size("tile")
    below = (district, lax.rem(tile + tiles - 1, tiles))
    above = (district, lax.rem(tile + 1, tiles))
    has_below = tile > 0
    has_above = tile < tiles - 1
    return below, above, has_below, has_above


def sort_pairs(keys, table, row):
    p = lax.broadcasted_iota(jnp.int32, (PAIRS, PAIRS), 0)
    q = lax.broadcasted_iota(jnp.int32, (PAIRS, PAIRS), 1)
    column = jnp.sum(jnp.where(p == q, keys, 0), axis=1, keepdims=True)
    ahead = jnp.logical_or(keys < column, jnp.logical_and(keys == column, q < p))
    rank = jnp.sum(jnp.where(ahead, 1, 0), axis=1, keepdims=True)
    table[row : row + 1, 0:PAIRS] = jnp.sum(jnp.where(rank == q, p, 0), axis=0, keepdims=True)
    lane = lax.broadcasted_iota(jnp.int32, (PAIRS, ROW), 1)
    table[row + 1 : row + 2, :] = jnp.sum(jnp.where(column <= lane, 1, 0), axis=0, keepdims=True)
    table[row + 2 : row + 3, :] = jnp.sum(jnp.where(column < lane, 1, 0), axis=0, keepdims=True)


def build_picks(rmap, count, picks):
    rows = lax.broadcasted_iota(jnp.int32, (ROW, ROW), 0)

    def block(o, carry):
        maps = rmap[0, pl.ds(pl.multiple_of(o * PB, PB), PB), :] + jnp.where(o < count, 0, 2 * ROW)
        for j in range(PB):
            picks[o * PB + j] = jnp.where(rows == maps[j : j + 1, :], 1.0, 0.0).astype(BF16)
        return carry

    lax.fori_loop(0, NB, block, 0)


def scatter_grads(picks, gt, ht):
    def step(i, carry):
        for j in range(UNROLL):
            product = jnp.dot(picks[i * UNROLL + j], gt[i * (UNROLL // PB) + j // PB], preferred_element_type=F32)
            ht[i * UNROLL + j] = product.astype(BF16)
        return carry

    lax.fori_loop(0, PAIRS // UNROLL, step, 0)


def gather_rows(picks, pin, ext, gathered):
    def step(i, carry):
        for j in range(UNROLL):
            p = i * UNROLL + j
            gathered[p] = jnp.dot(ext[pin[0, p]], picks[p], preferred_element_type=F32).astype(BF16)
        return carry

    lax.fori_loop(0, PAIRS // UNROLL, step, 0)


def running_sums(product, row, keys, table, sums):
    def step(i, carry):
        total, before = carry
        for j in range(UNROLL):
            at = i * UNROLL + j
            p = table[row, at]
            key = keys[0, p]
            total = total * jnp.where(key == before, 1.0, 0.0) + product(p)
            sums[at] = total
            before = key
        return total, before

    lax.fori_loop(0, PAIRS // UNROLL, step, (jnp.zeros((C, ROW), F32), jnp.int32(-1)))


def sum_of(key, row, table, sums):
    upto = table[row + 1, key]
    some = jnp.where(upto > table[row + 2, key], 1.0, 0.0)
    return sums[jnp.maximum(upto - 1, 0)] * some


def pack(table, sums, packed):
    lane = lax.broadcasted_iota(jnp.int32, (C, ROW), 1)

    def group(q, carry):
        a = sum_of(4 * q, 0, table, sums)
        b = pltpu.roll(sum_of(4 * q + 1, 0, table, sums), 96, 1)
        c = pltpu.roll(sum_of(4 * q + 2, 0, table, sums), 64, 1)
        d = pltpu.roll(sum_of(4 * q + 3, 0, table, sums), 32, 1)
        base = pl.multiple_of(q * 3 * C, 3 * C)
        packed[pl.ds(base, C), :] = jnp.where(lane < 96, a, b)
        packed[pl.ds(base + C, C), :] = jnp.where(lane < 64, b, c)
        packed[pl.ds(base + 2 * C, C), :] = jnp.where(lane < 32, c, d)
        return carry

    lax.fori_loop(0, 7, group, 0)
    packed[21 * C :, :] = jnp.zeros((PACKED - 21 * C, ROW), F32)


def fused_kernel(ny, nz, nx, *refs):
    (feat_in, pre_in, og_in, w1_in, w2_in, count_in, pin_in, poff_in, rmap_in, slo_in, shi_in,
     g1_ref, g2_ref, fg_ref,
     feat, pre, og, w1, w2, rmap, pin_v, poff_v, count, pin, poff, slo, shi, table_v, table,
     picks, gt, ht, gathered, sums, ext_h, ext_x, own,
     out_lo, out_hi, in_lo, in_hi, gb_lo, gb_hi, fb_lo, fb_hi, gb2_lo, gb2_hi, fb2_lo, fb2_hi,
     dwp, rcv0, snd1, rcv1, mine, gat3, fin1,
     load, tsem, hs, hr, gs, gr, g2s, g2r, s0, r0, s1, r1, s3, r3, s5, r5, s6, r6) = refs
    half = PACKED // 2
    district = lax.axis_index("district")
    tile = lax.axis_index("tile")
    core = lax.rem(district, 2)
    y = lax.div(district, 2)
    z = lax.div(tile, nx)
    x = lax.rem(tile, nx)
    below, above, has_below, has_above = tile_neighbours()
    other = (district + 1 - 2 * core, tile)

    def plane_of(n, me, device):
        steps = sorted(
            [(a, b) for a in range(n) for b in range(nx) if a + b],
            key=lambda step: -min(step[0], n - step[0]) - min(step[1], nx - step[1]),
        )
        places = [(lax.rem(me + a, n), lax.rem(x + b, nx)) for a, b in steps]
        return [i * nx + j for i, j in places], [device(i, j) for i, j in places]

    def line_of(n, me, device):
        order = sorted(range(1, n), key=lambda a: -min(a, n - a))
        return [device(lax.rem(me + a, n), x) for a in order]

    def over_y(i, j):
        return (i * 2 + core, z * nx + j)

    def over_z(i, j):
        return (district, i * nx + j)

    planes = (plane_of(ny, y, over_y), plane_of(nz, z, over_z))
    lines = (line_of(nz, z, over_z), line_of(ny, y, over_y))
    own_part = (y * nx + x, z * nx + x)
    own_slot = (z, y)
    parts = (half // (ny * nx), half // (nz * nx))
    slots = (nz, ny)

    loads = {}
    pieces = (("rmap", rmap_in, rmap), ("count", count_in, count), ("poff_v", poff_in, poff_v), ("pin_v", pin_in, pin_v),
              ("og", og_in, og), ("pin", pin_in, pin), ("poff", poff_in, poff), ("slo", slo_in, slo), ("shi", shi_in, shi),
              ("pre", pre_in, pre), ("feat", feat_in, feat), ("w2", w2_in, w2), ("w1", w1_in, w1))
    for i, (name, src, dst) in enumerate(pieces):
        loads[name] = pltpu.make_async_copy(src, dst, load.at[i])
        loads[name].start()
    barrier = pltpu.get_barrier_semaphore()
    peers = planes[0][1] + [other, below, above]
    peers += [over_z(lax.rem(z + a, nz), lax.rem(x + b, nx)) for a in range(1, nz) for b in range(nx)]
    for peer in peers:
        pl.semaphore_signal(barrier, inc=1, device_id=peer, device_id_type=pl.DeviceIdType.MESH)

    gt[...] = jnp.zeros_like(gt)
    table_v[...] = jnp.zeros_like(table_v)
    loads["poff_v"].wait()
    loads["pin_v"].wait()
    sort_pairs(poff_v[...], table_v, 0)
    sort_pairs(pin_v[...], table_v, 3)
    to_scalar = pltpu.make_async_copy(table_v, table, tsem)
    to_scalar.start()
    loads["rmap"].wait()
    loads["count"].wait()
    build_picks(rmap, count[0, 0], picks)
    loads["og"].wait()
    for b in range(NB):
        gt[b, :, 0:C] = jnp.transpose(og[b])
    scatter_grads(picks, gt, ht)

    for name in ("slo", "shi", "pre", "feat"):
        loads[name].wait()
    for j in range(KB):
        out_lo[0, j] = jnp.maximum(pre[slo[0, j]], 0.0)
        out_hi[0, j] = jnp.maximum(pre[shi[0, j]], 0.0)
        out_lo[1, j] = feat[slo[0, j]]
        out_hi[1, j] = feat[shi[0, j]]
    for name in ("pin", "poff", "w2"):
        loads[name].wait()
    to_scalar.wait()
    running_sums(
        lambda p: lax.dot_general(w2[poff[0, p]], ht[p, :, 0:C], NT, preferred_element_type=F32),
        3, pin, table, sums,
    )
    for j in range(KB):
        gb_lo[j] = sum_of(NB + j, 3, table, sums).astype(gb_lo.dtype)
        gb_hi[j] = sum_of(NB + KB + j, 3, table, sums).astype(gb_hi.dtype)
    for b in range(NB):
        own[b] = sum_of(b, 3, table, sums)
    pl.semaphore_wait(barrier, len(peers))
    halo = []
    for f in range(2):
        halo.append((
            remote(out_hi.at[f], in_lo.at[f], hs.at[0, f], hr.at[0, f], above),
            remote(out_lo.at[f], in_hi.at[f], hs.at[1, f], hr.at[1, f], below),
        ))
    back = (
        remote(gb_hi, fb_lo, gs.at[0], gr.at[0], above),
        remote(gb_lo, fb_hi, gs.at[1], gr.at[1], below),
    )
    for copy in list(halo[1]) + list(back) + list(halo[0]):
        copy.start()

    def extend(f, own, ext):
        ext[0:NB] = own
        halo[f][0].wait()
        ext[NB : NB + KB] = jnp.where(has_below, in_lo[f], jnp.zeros_like(in_lo[f]))
        halo[f][1].wait()
        ext[NB + KB :] = jnp.where(has_above, in_hi[f], jnp.zeros_like(in_hi[f]))

    keep = pl.ds(pl.multiple_of(core * half, half), half)
    away = pl.ds(pl.multiple_of((1 - core) * half, half), half)
    chunks = [pl.ds(pl.multiple_of(own_part[g] * parts[g], parts[g]), parts[g]) for g in range(2)]
    outs = (g1_ref, g2_ref)

    def swap_halves(g):
        remote(dwp.at[g, away, :], rcv0.at[g], s0.at[g], r0.at[g], other).start()

    def scatter_plane(g):
        wait_all(rcv0.at[g], r0.at[g])
        snd1[g] = (dwp[g, keep, :] + rcv0[g]).astype(BF16)
        part = parts[g]
        for s, (index, peer) in enumerate(zip(*planes[g])):
            rows = pl.ds(pl.multiple_of(index * part, part), part)
            remote(snd1.at[g, rows, :], rcv1.at[g, s, 0:part], s1.at[g], r1.at[g], peer).start()
        at = pl.ds(pl.multiple_of(core * half + own_part[g] * part, part), part)
        mine[g, 0:part] = dwp[g, at, :] + rcv0[g, chunks[g], :]

    def exchange_line(g):
        part = parts[g]
        near = half // part - 1
        wait_all(rcv1.at[g, 0:near, 0:part], r1.at[g])
        total = mine[g, 0:part]
        for s in range(near):
            total = total + rcv1[g, s, 0:part].astype(F32)
        gat3[g, own_slot[g], 0:part] = total.astype(BF16)
        for peer in lines[g]:
            block = gat3.at[g, own_slot[g], 0:part]
            remote(block, block, s3.at[g], r3.at[g], peer).start()

    def gather_plane(g):
        part = parts[g]
        wait_all(gat3.at[g, 0 : slots[g] - 1, 0:part], r3.at[g])
        total = gat3[g, 0, 0:part].astype(F32)
        for i in range(1, slots[g]):
            total = total + gat3[g, i, 0:part].astype(F32)
        fin1[g, chunks[g], :] = total.astype(BF16)
        block = fin1.at[g, chunks[g], :]
        for peer in planes[g][1]:
            remote(block, block, s5.at[g], r5.at[g], peer).start()

    def share_halves(g):
        wait_all(fin1.at[g, 0 : half - parts[g]], r5.at[g])
        remote(fin1.at[g], outs[g].at[keep, :], s6.at[g], r6.at[g], other).start()
        outs[g][keep, :] = fin1[g]

    def settle(g):
        wait_all(rcv0.at[g], s0.at[g])
        wait_all(snd1.at[g, 0 : half - parts[g]], s1.at[g])
        wait_all(gat3.at[g, 0 : slots[g] - 1, 0 : parts[g]], s3.at[g])
        wait_all(fin1.at[g, 0 : half - parts[g]], s5.at[g])
        wait_all(fin1.at[g], s6.at[g])
        wait_all(fin1.at[g], r6.at[g])

    def add_back(b, total, lo, hi):
        for j in range(KB):
            from_below = jnp.where(jnp.logical_and(slo[0, j] == b, has_below), 1.0, 0.0)
            from_above = jnp.where(jnp.logical_and(shi[0, j] == b, has_above), 1.0, 0.0)
            total = total + from_below * lo[j].astype(F32) + from_above * hi[j].astype(F32)
        return total

    extend(1, feat[...], ext_x)
    gather_rows(picks, pin, ext_x, gathered)
    for copy in back:
        copy.wait()
    for b in range(NB):
        hidden_grad = add_back(b, own[b], fb_lo, fb_hi)
        gt[b, :, 0:C] = jnp.transpose(jnp.where(pre[b] > 0, hidden_grad, 0.0).astype(BF16))
    running_sums(
        lambda p: jnp.dot(gathered[p], gt[p // PB], preferred_element_type=F32), 0, poff, table, sums
    )
    pack(table, sums, dwp.at[0])
    swap_halves(0)

    extend(0, jnp.maximum(pre[...], 0.0), ext_h)
    running_sums(
        lambda p: jnp.dot(ext_h[pin[0, p]], ht[p], preferred_element_type=F32), 0, poff, table, sums
    )
    pack(table, sums, dwp.at[1])
    swap_halves(1)
    scatter_plane(0)
    scatter_plane(1)

    scatter_grads(picks, gt, ht)
    loads["w1"].wait()
    running_sums(
        lambda p: lax.dot_general(w1[poff[0, p]], ht[p, :, 0:C], NT, preferred_element_type=F32),
        3, pin, table, sums,
    )
    for j in range(KB):
        gb2_lo[j] = sum_of(NB + j, 3, table, sums)
        gb2_hi[j] = sum_of(NB + KB + j, 3, table, sums)
    for b in range(NB):
        own[b] = sum_of(b, 3, table, sums)

    exchange_line(0)
    exchange_line(1)
    last = (
        remote(gb2_hi, fb2_lo, g2s.at[0], g2r.at[0], above),
        remote(gb2_lo, fb2_hi, g2s.at[1], g2r.at[1], below),
    )
    for copy in last:
        copy.start()
    gather_plane(0)
    gather_plane(1)
    for copy in last:
        copy.wait()
    for b in range(NB):
        fg_ref[b] = add_back(b, own[b], fb2_lo, fb2_hi).astype(BF16)
    share_halves(0)
    share_halves(1)
    settle(0)
    settle(1)


def fused(ny, nz, nx, *operands):
    half = PACKED // 2
    part = half // (min(ny, nz) * nx)
    most = max(ny, nz)
    near = most * nx - 1
    dma = pltpu.SemaphoreType.DMA
    packed = jax.ShapeDtypeStruct((PACKED, ROW), BF16)
    blocks = jax.ShapeDtypeStruct((NB, C, ROW), BF16)
    four = pltpu.VMEM((NB, C, ROW), BF16)
    four_wide = pltpu.VMEM((NB, C, ROW), F32)
    kernel_weights = pltpu.VMEM((K, C, C), BF16)
    return pl.pallas_call(
        functools.partial(fused_kernel, ny, nz, nx),
        out_shape=(packed, packed, blocks),
        in_specs=[HBM] * 11,
        out_specs=(VMEM,) * 3,
        scratch_shapes=[
            four, four, four, kernel_weights, kernel_weights,
            pltpu.VMEM((1, PAIRS, ROW), jnp.int32),
            pltpu.VMEM((1, PAIRS), jnp.int32),
            pltpu.VMEM((1, PAIRS), jnp.int32),
            pltpu.SMEM((1, 1), jnp.int32),
            pltpu.SMEM((1, PAIRS), jnp.int32),
            pltpu.SMEM((1, PAIRS), jnp.int32),
            pltpu.SMEM((1, KB), jnp.int32),
            pltpu.SMEM((1, KB), jnp.int32),
            pltpu.VMEM((8, ROW), jnp.int32),
            pltpu.SMEM((8, ROW), jnp.int32),
            pltpu.VMEM((PAIRS, ROW, ROW), BF16),
            pltpu.VMEM((NB, ROW, ROW), BF16),
            pltpu.VMEM((PAIRS, ROW, ROW), BF16),
            pltpu.VMEM((PAIRS, C, ROW), BF16),
            pltpu.VMEM((PAIRS, C, ROW), F32),
            pltpu.VMEM((EXT, C, ROW), BF16),
            pltpu.VMEM((EXT, C, ROW), BF16),
            four_wide,
            pltpu.VMEM((2, KB, C, ROW), BF16),
            pltpu.VMEM((2, KB, C, ROW), BF16),
            pltpu.VMEM((2, KB, C, ROW), BF16),
            pltpu.VMEM((2, KB, C, ROW), BF16),
            four, four, four, four, four_wide, four_wide, four_wide, four_wide,
            pltpu.VMEM((2, PACKED, ROW), F32),
            pltpu.VMEM((2, half, ROW), F32),
            pltpu.VMEM((2, half, ROW), BF16),
            pltpu.VMEM((2, near, part, ROW), BF16),
            pltpu.VMEM((2, part, ROW), F32),
            pltpu.VMEM((2, most, part, ROW), BF16),
            pltpu.VMEM((2, half, ROW), BF16),
            dma((13,)), dma,
            dma((2, 2)), dma((2, 2)),
            dma((2,)), dma((2,)),
            dma((2,)), dma((2,)),
            dma((2,)), dma((2,)),
            dma((2,)), dma((2,)),
            dma((2,)), dma((2,)),
            dma((2,)), dma((2,)),
            dma((2,)), dma((2,)),
        ],
        compiler_params=pltpu.CompilerParams(
            collective_id=0, has_side_effects=True, vmem_limit_bytes=VMEM_LIMIT
        ),
        name="fused",
    )(*operands)


def finish_kernel(grad_ref, g1_ref, g2_ref, fg_ref, w1_ref, w2_ref, wide, sems, last):
    lane = lax.broadcasted_iota(jnp.int32, (C, ROW), 1)
    first = pltpu.make_async_copy(grad_ref, fg_ref, last)
    first.start()
    copies = [first]
    for g, (src, dst) in enumerate(((g1_ref, w1_ref), (g2_ref, w2_ref))):
        for q in range(7):
            base = q * 3 * C
            size = min(4, K - 4 * q)
            r1 = src[base : base + C, :].astype(F32)
            r2 = src[base + C : base + 2 * C, :].astype(F32)
            r3 = src[base + 2 * C : base + 3 * C, :].astype(F32)
            wide[g, 4 * q] = r1[:, 0:C]
            wide[g, 4 * q + 1] = pltpu.roll(jnp.where(lane < 96, r2, r1), 32, 1)[:, 0:C]
            wide[g, 4 * q + 2] = pltpu.roll(jnp.where(lane < 64, r3, r2), 64, 1)[:, 0:C]
            if size == 4:
                wide[g, 4 * q + 3] = pltpu.roll(r3, 96, 1)[:, 0:C]
            copy = pltpu.make_async_copy(
                wide.at[g, pl.ds(4 * q, size)], dst.at[pl.ds(4 * q, size)], sems.at[g, q]
            )
            copy.start()
            copies.append(copy)
    for copy in copies:
        copy.wait()


def finish(grad, g1, g2):
    kern = jax.ShapeDtypeStruct((K, C, C), F32)
    return pl.pallas_call(
        finish_kernel,
        out_shape=(jax.ShapeDtypeStruct((NB, C, ROW), BF16), kern, kern),
        in_specs=[VMEM] * 3,
        out_specs=(HBM,) * 3,
        scratch_shapes=[
            pltpu.VMEM((2, K, C, C), F32),
            pltpu.SemaphoreType.DMA((2, 7)),
            pltpu.SemaphoreType.DMA,
        ],
        compiler_params=pltpu.CompilerParams(vmem_limit_bytes=VMEM_LIMIT),
        name="finish",
    )(grad, g1, g2)


def body(ny, nz, nx, features, pre_act, out_grad, weight_one, weight_two, block_count, pair_in, pair_off,
         row_map, send_lo, send_hi):
    operands = (features, pre_act, out_grad, weight_one, weight_two, block_count.reshape(1, 1), pair_in, pair_off,
                row_map, send_lo, send_hi)
    operands = [a if a.size == 1 else pltpu.with_memory_space_constraint(a, pltpu.HBM) for a in operands]
    g1, g2, grad = fused(ny, nz, nx, *operands)
    return finish(grad, g1, g2)


def solution(mesh):
    placed = (
        P(("district", "tile"), None, None),
        P(("district", "tile"), None, None),
        P(("district", "tile"), None, None),
        P(),
        P(),
        P(("district", "tile")),
        P(("district", "tile"), None),
        P(("district", "tile"), None),
        P(("district", "tile"), None, None),
        P(("district", "tile"), None),
        P(("district", "tile"), None),
    )
    tiles = mesh.shape["tile"]
    nx = 4 if tiles % 4 == 0 and tiles > 4 else 2
    ny, nz = mesh.shape["district"] // 2, tiles // nx
    return jax.shard_map(
        functools.partial(body, ny, nz, nx),
        mesh=mesh,
        in_specs=placed,
        out_specs=(P(("district", "tile"), None, None), P(), P()),
        check_vma=False,
    )
```

```python
import functools

import jax
import jax.numpy as jnp
from jax import lax
from jax.experimental import pallas as pl
from jax.experimental.pallas import tpu as pltpu
from jax.sharding import PartitionSpec as P

K = 27
PB = 16
NB = 4
KB = 4
C = 96
ROW = 128
EXT = NB + 2 * KB
PAIRS = NB * PB
UNROLL = 64
NT = (((1,), (1,)), ((), ()))
PACKED = 2048
F32 = jnp.float32
BF16 = jnp.bfloat16
VMEM_LIMIT = 28 * 1024 * 1024

HBM = pl.BlockSpec(memory_space=pltpu.HBM)
VMEM = pl.BlockSpec(memory_space=pltpu.VMEM)


def remote(src, dst, send_sem, recv_sem, where):
    return pltpu.make_async_remote_copy(
        src_ref=src,
        dst_ref=dst,
        send_sem=send_sem,
        recv_sem=recv_sem,
        device_id=where,
        device_id_type=pl.DeviceIdType.MESH,
    )


def wait_all(like, sem):
    pltpu.make_async_copy(like, like, sem).wait()


def tile_neighbours():
    district = lax.axis_index("district")
    tile = lax.axis_index("tile")
    tiles = lax.axis_size("tile")
    below = (district, lax.rem(tile + tiles - 1, tiles))
    above = (district, lax.rem(tile + 1, tiles))
    has_below = tile > 0
    has_above = tile < tiles - 1
    return below, above, has_below, has_above


def sort_pairs(keys, table, row):
    p = lax.broadcasted_iota(jnp.int32, (PAIRS, PAIRS), 0)
    q = lax.broadcasted_iota(jnp.int32, (PAIRS, PAIRS), 1)
    column = jnp.sum(jnp.where(p == q, keys, 0), axis=1, keepdims=True)
    ahead = jnp.logical_or(keys < column, jnp.logical_and(keys == column, q < p))
    rank = jnp.sum(jnp.where(ahead, 1, 0), axis=1, keepdims=True)
    table[row : row + 1, 0:PAIRS] = jnp.sum(jnp.where(rank == q, p, 0), axis=0, keepdims=True)
    lane = lax.broadcasted_iota(jnp.int32, (PAIRS, ROW), 1)
    table[row + 1 : row + 2, :] = jnp.sum(jnp.where(column <= lane, 1, 0), axis=0, keepdims=True)
    table[row + 2 : row + 3, :] = jnp.sum(jnp.where(column < lane, 1, 0), axis=0, keepdims=True)


def build_picks(rmap, count, picks):
    rows = lax.broadcasted_iota(jnp.int32, (ROW, ROW), 0)

    def block(o, carry):
        maps = rmap[0, pl.ds(pl.multiple_of(o * PB, PB), PB), :] + jnp.where(o < count, 0, 2 * ROW)
        for j in range(PB):
            picks[o * PB + j] = jnp.where(rows == maps[j : j + 1, :], 1.0, 0.0).astype(BF16)
        return carry

    lax.fori_loop(0, NB, block, 0)


def scatter_columns(rmap, count, grads, h):
    lane = lax.broadcasted_iota(jnp.int32, (ROW, ROW), 1)
    pair = lax.broadcasted_iota(jnp.int32, (PAIRS, ROW), 0)
    columns = jnp.transpose(rmap[0] + jnp.where(pair < count * PB, 0, 2 * ROW))
    for p in range(PAIRS):
        picks = jnp.where(columns[:, p : p + 1] == lane, 1.0, 0.0).astype(BF16)
        h[p] = jnp.dot(grads[p // PB], picks, preferred_element_type=F32).astype(BF16)


def scatter_grads(picks, gt, ht):
    def step(i, carry):
        for j in range(UNROLL):
            product = jnp.dot(picks[i * UNROLL + j], gt[i * (UNROLL // PB) + j // PB], preferred_element_type=F32)
            ht[i * UNROLL + j] = product.astype(BF16)
        return carry

    lax.fori_loop(0, PAIRS // UNROLL, step, 0)


def gather_rows(picks, pin, ext, gathered):
    def step(i, carry):
        for j in range(UNROLL):
            p = i * UNROLL + j
            gathered[p] = jnp.dot(ext[pin[0, p]], picks[p], preferred_element_type=F32).astype(BF16)
        return carry

    lax.fori_loop(0, PAIRS // UNROLL, step, 0)


def running_sums(product, row, keys, table, sums):
    def step(i, carry):
        total, before = carry
        for j in range(UNROLL):
            at = i * UNROLL + j
            p = table[row, at]
            key = keys[0, p]
            total = total * jnp.where(key == before, 1.0, 0.0) + product(p)
            sums[at] = total
            before = key
        return total, before

    lax.fori_loop(0, PAIRS // UNROLL, step, (jnp.zeros((C, ROW), F32), jnp.int32(-1)))


def sum_of(key, row, table, sums):
    upto = table[row + 1, key]
    some = jnp.where(upto > table[row + 2, key], 1.0, 0.0)
    return sums[jnp.maximum(upto - 1, 0)] * some


def pack(table, sums, packed):
    lane = lax.broadcasted_iota(jnp.int32, (C, ROW), 1)

    for q in range(7):
        a = sum_of(4 * q, 0, table, sums)
        b = pltpu.roll(sum_of(4 * q + 1, 0, table, sums), 96, 1)
        c = pltpu.roll(sum_of(4 * q + 2, 0, table, sums), 64, 1)
        d = pltpu.roll(sum_of(4 * q + 3, 0, table, sums), 32, 1)
        base = q * 3 * C
        packed[pl.ds(base, C), :] = jnp.where(lane < 96, a, b)
        packed[pl.ds(base + C, C), :] = jnp.where(lane < 64, b, c)
        packed[pl.ds(base + 2 * C, C), :] = jnp.where(lane < 32, c, d)
    packed[21 * C :, :] = jnp.zeros((PACKED - 21 * C, ROW), F32)


def fused_kernel(ny, nz, nx, *refs):
    (feat_in, pre_in, og_in, w1_in, w2_in, count_in, pin_in, poff_in, rmap_in, slo_in, shi_in,
     g1_ref, g2_ref, fg_ref,
     feat, pre, og, w1, w2, rmap, pin_v, poff_v, count, pin, poff, slo, shi, table_v, table,
     picks, gt, ht, gathered, sums, ext_h, ext_x, own,
     out_lo, out_hi, in_lo, in_hi, gb_lo, gb_hi, fb_lo, fb_hi, gb2_lo, gb2_hi, fb2_lo, fb2_hi,
     dwp, rcv0, snd1, rcv1, mine, gat3, fin1,
     load, tsem, hs, hr, gs, gr, g2s, g2r, s0, r0, s1, r1, s3, r3, s5, r5, s6, r6) = refs
    half = PACKED // 2
    district = lax.axis_index("district")
    tile = lax.axis_index("tile")
    core = lax.rem(district, 2)
    y = lax.div(district, 2)
    z = lax.div(tile, nx)
    x = lax.rem(tile, nx)
    below, above, has_below, has_above = tile_neighbours()
    other = (district + 1 - 2 * core, tile)

    def plane_of(n, me, device):
        steps = sorted(
            [(a, b) for a in range(n) for b in range(nx) if a + b],
            key=lambda step: -min(step[0], n - step[0]) - min(step[1], nx - step[1]),
        )
        places = [(lax.rem(me + a, n), lax.rem(x + b, nx)) for a, b in steps]
        return [i * nx + j for i, j in places], [device(i, j) for i, j in places]

    def line_of(n, me, device):
        order = sorted(range(1, n), key=lambda a: -min(a, n - a))
        return [device(lax.rem(me + a, n), x) for a in order]

    def over_y(i, j):
        return (i * 2 + core, z * nx + j)

    def over_z(i, j):
        return (district, i * nx + j)

    planes = (plane_of(ny, y, over_y), plane_of(nz, z, over_z))
    lines = (line_of(nz, z, over_z), line_of(ny, y, over_y))
    own_part = (y * nx + x, z * nx + x)
    own_slot = (z, y)
    parts = (half // (ny * nx), half // (nz * nx))
    slots = (nz, ny)

    loads = {}
    pieces = (("rmap", rmap_in, rmap), ("count", count_in, count), ("poff_v", poff_in, poff_v), ("pin_v", pin_in, pin_v),
              ("og", og_in, og), ("pin", pin_in, pin), ("poff", poff_in, poff), ("slo", slo_in, slo), ("shi", shi_in, shi),
              ("pre", pre_in, pre), ("feat", feat_in, feat), ("w2", w2_in, w2), ("w1", w1_in, w1))
    for i, (name, src, dst) in enumerate(pieces):
        loads[name] = pltpu.make_async_copy(src, dst, load.at[i])
        loads[name].start()
    barrier = pltpu.get_barrier_semaphore()
    peers = planes[0][1] + [other, below, above]
    peers += [over_z(lax.rem(z + a, nz), lax.rem(x + b, nx)) for a in range(1, nz) for b in range(nx)]
    for peer in peers:
        pl.semaphore_signal(barrier, inc=1, device_id=peer, device_id_type=pl.DeviceIdType.MESH)

    gt[...] = jnp.zeros_like(gt)
    table_v[...] = jnp.zeros_like(table_v)
    loads["poff_v"].wait()
    loads["pin_v"].wait()
    sort_pairs(poff_v[...], table_v, 0)
    sort_pairs(pin_v[...], table_v, 3)
    to_scalar = pltpu.make_async_copy(table_v, table, tsem)
    to_scalar.start()
    loads["rmap"].wait()
    loads["count"].wait()
    loads["og"].wait()
    scatter_columns(rmap, count[0, 0], og, gathered)

    for name in ("slo", "shi", "pre", "feat"):
        loads[name].wait()
    for j in range(KB):
        out_lo[0, j] = jnp.maximum(pre[slo[0, j]], 0.0)
        out_hi[0, j] = jnp.maximum(pre[shi[0, j]], 0.0)
        out_lo[1, j] = feat[slo[0, j]]
        out_hi[1, j] = feat[shi[0, j]]
    for name in ("pin", "poff", "w2"):
        loads[name].wait()
    to_scalar.wait()
    running_sums(
        lambda p: jnp.dot(w2[poff[0, p]], gathered[p], preferred_element_type=F32),
        3, pin, table, sums,
    )
    for j in range(KB):
        gb_lo[j] = sum_of(NB + j, 3, table, sums).astype(gb_lo.dtype)
        gb_hi[j] = sum_of(NB + KB + j, 3, table, sums).astype(gb_hi.dtype)
    for b in range(NB):
        own[b] = sum_of(b, 3, table, sums)
    pl.semaphore_wait(barrier, len(peers))
    halo = []
    for f in range(2):
        halo.append((
            remote(out_hi.at[f], in_lo.at[f], hs.at[0, f], hr.at[0, f], above),
            remote(out_lo.at[f], in_hi.at[f], hs.at[1, f], hr.at[1, f], below),
        ))
    back = (
        remote(gb_hi, fb_lo, gs.at[0], gr.at[0], above),
        remote(gb_lo, fb_hi, gs.at[1], gr.at[1], below),
    )
    for copy in list(halo[1]) + list(back) + list(halo[0]):
        copy.start()

    build_picks(rmap, count[0, 0], picks)
    for b in range(NB):
        gt[b, :, 0:C] = jnp.transpose(og[b])
    scatter_grads(picks, gt, ht)

    def extend(f, own, ext):
        ext[0:NB] = own
        halo[f][0].wait()
        ext[NB : NB + KB] = jnp.where(has_below, in_lo[f], jnp.zeros_like(in_lo[f]))
        halo[f][1].wait()
        ext[NB + KB :] = jnp.where(has_above, in_hi[f], jnp.zeros_like(in_hi[f]))

    keep = pl.ds(pl.multiple_of(core * half, half), half)
    away = pl.ds(pl.multiple_of((1 - core) * half, half), half)
    chunks = [pl.ds(pl.multiple_of(own_part[g] * parts[g], parts[g]), parts[g]) for g in range(2)]
    outs = (g1_ref, g2_ref)

    def swap_halves(g):
        remote(dwp.at[g, away, :], rcv0.at[g], s0.at[g], r0.at[g], other).start()

    def scatter_plane(g):
        wait_all(rcv0.at[g], r0.at[g])
        snd1[g] = (dwp[g, keep, :] + rcv0[g]).astype(BF16)
        part = parts[g]
        for s, (index, peer) in enumerate(zip(*planes[g])):
            rows = pl.ds(pl.multiple_of(index * part, part), part)
            remote(snd1.at[g, rows, :], rcv1.at[g, s, 0:part], s1.at[g], r1.at[g], peer).start()
        at = pl.ds(pl.multiple_of(core * half + own_part[g] * part, part), part)
        mine[g, 0:part] = dwp[g, at, :] + rcv0[g, chunks[g], :]

    def exchange_line(g):
        part = parts[g]
        near = half // part - 1
        wait_all(rcv1.at[g, 0:near, 0:part], r1.at[g])
        total = mine[g, 0:part]
        for s in range(near):
            total = total + rcv1[g, s, 0:part].astype(F32)
        gat3[g, own_slot[g], 0:part] = total.astype(BF16)
        for peer in lines[g]:
            block = gat3.at[g, own_slot[g], 0:part]
            remote(block, block, s3.at[g], r3.at[g], peer).start()

    def gather_plane(g):
        part = parts[g]
        wait_all(gat3.at[g, 0 : slots[g] - 1, 0:part], r3.at[g])
        total = gat3[g, 0, 0:part].astype(F32)
        for i in range(1, slots[g]):
            total = total + gat3[g, i, 0:part].astype(F32)
        fin1[g, chunks[g], :] = total.astype(BF16)
        block = fin1.at[g, chunks[g], :]
        for peer in planes[g][1]:
            remote(block, block, s5.at[g], r5.at[g], peer).start()

    def share_halves(g):
        wait_all(fin1.at[g, 0 : half - parts[g]], r5.at[g])
        remote(fin1.at[g], outs[g].at[keep, :], s6.at[g], r6.at[g], other).start()
        outs[g][keep, :] = fin1[g]

    def settle(g):
        wait_all(rcv0.at[g], s0.at[g])
        wait_all(snd1.at[g, 0 : half - parts[g]], s1.at[g])
        wait_all(gat3.at[g, 0 : slots[g] - 1, 0 : parts[g]], s3.at[g])
        wait_all(fin1.at[g, 0 : half - parts[g]], s5.at[g])
        wait_all(fin1.at[g], s6.at[g])
        wait_all(fin1.at[g], r6.at[g])

    def add_back(b, total, lo, hi):
        for j in range(KB):
            from_below = jnp.where(jnp.logical_and(slo[0, j] == b, has_below), 1.0, 0.0)
            from_above = jnp.where(jnp.logical_and(shi[0, j] == b, has_above), 1.0, 0.0)
            total = total + from_below * lo[j].astype(F32) + from_above * hi[j].astype(F32)
        return total

    extend(1, feat[...], ext_x)
    gather_rows(picks, pin, ext_x, gathered)
    for copy in back:
        copy.wait()
    for b in range(NB):
        hidden_grad = add_back(b, own[b], fb_lo, fb_hi)
        gt[b, :, 0:C] = jnp.transpose(jnp.where(pre[b] > 0, hidden_grad, 0.0).astype(BF16))
    running_sums(
        lambda p: jnp.dot(gathered[p], gt[p // PB], preferred_element_type=F32), 0, poff, table, sums
    )
    pack(table, sums, dwp.at[0])
    swap_halves(0)

    extend(0, jnp.maximum(pre[...], 0.0), ext_h)
    running_sums(
        lambda p: jnp.dot(ext_h[pin[0, p]], ht[p], preferred_element_type=F32), 0, poff, table, sums
    )
    pack(table, sums, dwp.at[1])
    swap_halves(1)
    scatter_plane(0)
    scatter_plane(1)

    scatter_grads(picks, gt, ht)
    loads["w1"].wait()
    running_sums(
        lambda p: lax.dot_general(w1[poff[0, p]], ht[p, :, 0:C], NT, preferred_element_type=F32),
        3, pin, table, sums,
    )
    for j in range(KB):
        gb2_lo[j] = sum_of(NB + j, 3, table, sums)
        gb2_hi[j] = sum_of(NB + KB + j, 3, table, sums)
    for b in range(NB):
        own[b] = sum_of(b, 3, table, sums)

    exchange_line(0)
    exchange_line(1)
    last = (
        remote(gb2_hi, fb2_lo, g2s.at[0], g2r.at[0], above),
        remote(gb2_lo, fb2_hi, g2s.at[1], g2r.at[1], below),
    )
    for copy in last:
        copy.start()
    gather_plane(0)
    gather_plane(1)
    for copy in last:
        copy.wait()
    for b in range(NB):
        fg_ref[b] = add_back(b, own[b], fb2_lo, fb2_hi).astype(BF16)
    share_halves(0)
    share_halves(1)
    settle(0)
    settle(1)


def fused(ny, nz, nx, *operands):
    half = PACKED // 2
    part = half // (min(ny, nz) * nx)
    most = max(ny, nz)
    near = most * nx - 1
    dma = pltpu.SemaphoreType.DMA
    packed = jax.ShapeDtypeStruct((PACKED, ROW), BF16)
    blocks = jax.ShapeDtypeStruct((NB, C, ROW), BF16)
    four = pltpu.VMEM((NB, C, ROW), BF16)
    four_wide = pltpu.VMEM((NB, C, ROW), F32)
    kernel_weights = pltpu.VMEM((K, C, C), BF16)
    return pl.pallas_call(
        functools.partial(fused_kernel, ny, nz, nx),
        out_shape=(packed, packed, blocks),
        in_specs=[HBM] * 11,
        out_specs=(VMEM,) * 3,
        scratch_shapes=[
            four, four, four, kernel_weights, kernel_weights,
            pltpu.VMEM((1, PAIRS, ROW), jnp.int32),
            pltpu.VMEM((1, PAIRS), jnp.int32),
            pltpu.VMEM((1, PAIRS), jnp.int32),
            pltpu.SMEM((1, 1), jnp.int32),
            pltpu.SMEM((1, PAIRS), jnp.int32),
            pltpu.SMEM((1, PAIRS), jnp.int32),
            pltpu.SMEM((1, KB), jnp.int32),
            pltpu.SMEM((1, KB), jnp.int32),
            pltpu.VMEM((8, ROW), jnp.int32),
            pltpu.SMEM((8, ROW), jnp.int32),
            pltpu.VMEM((PAIRS, ROW, ROW), BF16),
            pltpu.VMEM((NB, ROW, ROW), BF16),
            pltpu.VMEM((PAIRS, ROW, ROW), BF16),
            pltpu.VMEM((PAIRS, C, ROW), BF16),
            pltpu.VMEM((PAIRS, C, ROW), F32),
            pltpu.VMEM((EXT, C, ROW), BF16),
            pltpu.VMEM((EXT, C, ROW), BF16),
            four_wide,
            pltpu.VMEM((2, KB, C, ROW), BF16),
            pltpu.VMEM((2, KB, C, ROW), BF16),
            pltpu.VMEM((2, KB, C, ROW), BF16),
            pltpu.VMEM((2, KB, C, ROW), BF16),
            four, four, four, four, four_wide, four_wide, four_wide, four_wide,
            pltpu.VMEM((2, PACKED, ROW), F32),
            pltpu.VMEM((2, half, ROW), F32),
            pltpu.VMEM((2, half, ROW), BF16),
            pltpu.VMEM((2, near, part, ROW), BF16),
            pltpu.VMEM((2, part, ROW), F32),
            pltpu.VMEM((2, most, part, ROW), BF16),
            pltpu.VMEM((2, half, ROW), BF16),
            dma((13,)), dma,
            dma((2, 2)), dma((2, 2)),
            dma((2,)), dma((2,)),
            dma((2,)), dma((2,)),
            dma((2,)), dma((2,)),
            dma((2,)), dma((2,)),
            dma((2,)), dma((2,)),
            dma((2,)), dma((2,)),
            dma((2,)), dma((2,)),
        ],
        compiler_params=pltpu.CompilerParams(
            collective_id=0, has_side_effects=True, vmem_limit_bytes=VMEM_LIMIT
        ),
        name="fused",
    )(*operands)


def finish_kernel(grad_ref, g1_ref, g2_ref, fg_ref, w1_ref, w2_ref, wide, sems, last):
    lane = lax.broadcasted_iota(jnp.int32, (C, ROW), 1)
    first = pltpu.make_async_copy(grad_ref, fg_ref, last)
    first.start()
    copies = [first]
    for g, (src, dst) in enumerate(((g1_ref, w1_ref), (g2_ref, w2_ref))):
        for q in range(7):
            base = q * 3 * C
            size = min(4, K - 4 * q)
            r1 = src[base : base + C, :].astype(F32)
            r2 = src[base + C : base + 2 * C, :].astype(F32)
            r3 = src[base + 2 * C : base + 3 * C, :].astype(F32)
            wide[g, 4 * q] = r1[:, 0:C]
            wide[g, 4 * q + 1] = pltpu.roll(jnp.where(lane < 96, r2, r1), 32, 1)[:, 0:C]
            wide[g, 4 * q + 2] = pltpu.roll(jnp.where(lane < 64, r3, r2), 64, 1)[:, 0:C]
            if size == 4:
                wide[g, 4 * q + 3] = pltpu.roll(r3, 96, 1)[:, 0:C]
            copy = pltpu.make_async_copy(
                wide.at[g, pl.ds(4 * q, size)], dst.at[pl.ds(4 * q, size)], sems.at[g, q]
            )
            copy.start()
            copies.append(copy)
    for copy in copies:
        copy.wait()


def finish(grad, g1, g2):
    kern = jax.ShapeDtypeStruct((K, C, C), F32)
    return pl.pallas_call(
        finish_kernel,
        out_shape=(jax.ShapeDtypeStruct((NB, C, ROW), BF16), kern, kern),
        in_specs=[VMEM] * 3,
        out_specs=(HBM,) * 3,
        scratch_shapes=[
            pltpu.VMEM((2, K, C, C), F32),
            pltpu.SemaphoreType.DMA((2, 7)),
            pltpu.SemaphoreType.DMA,
        ],
        compiler_params=pltpu.CompilerParams(vmem_limit_bytes=VMEM_LIMIT),
        name="finish",
    )(grad, g1, g2)


def body(ny, nz, nx, features, pre_act, out_grad, weight_one, weight_two, block_count, pair_in, pair_off,
         row_map, send_lo, send_hi):
    operands = (features, pre_act, out_grad, weight_one, weight_two, block_count.reshape(1, 1), pair_in, pair_off,
                row_map, send_lo, send_hi)
    operands = [a if a.size == 1 else pltpu.with_memory_space_constraint(a, pltpu.HBM) for a in operands]
    g1, g2, grad = fused(ny, nz, nx, *operands)
    return finish(grad, g1, g2)


def solution(mesh):
    placed = (
        P(("district", "tile"), None, None),
        P(("district", "tile"), None, None),
        P(("district", "tile"), None, None),
        P(),
        P(),
        P(("district", "tile")),
        P(("district", "tile"), None),
        P(("district", "tile"), None),
        P(("district", "tile"), None, None),
        P(("district", "tile"), None),
        P(("district", "tile"), None),
    )
    tiles = mesh.shape["tile"]
    nx = 4 if tiles % 4 == 0 and tiles > 4 else 2
    ny, nz = mesh.shape["district"] // 2, tiles // nx
    return jax.shard_map(
        functools.partial(body, ny, nz, nx),
        mesh=mesh,
        in_specs=placed,
        out_specs=(P(("district", "tile"), None, None), P(), P()),
        check_vma=False,
    )
```

```python
import functools

import jax
import jax.numpy as jnp
from jax import lax
from jax.experimental import pallas as pl
from jax.experimental.pallas import tpu as pltpu
from jax.sharding import PartitionSpec as P

K = 27
PB = 16
NB = 4
KB = 4
C = 96
ROW = 128
EXT = NB + 2 * KB
PAIRS = NB * PB
UNROLL = 64
NT = (((1,), (1,)), ((), ()))
PACKED = 2048
F32 = jnp.float32
BF16 = jnp.bfloat16
VMEM_LIMIT = 28 * 1024 * 1024

HBM = pl.BlockSpec(memory_space=pltpu.HBM)
VMEM = pl.BlockSpec(memory_space=pltpu.VMEM)


def remote(src, dst, send_sem, recv_sem, where):
    return pltpu.make_async_remote_copy(
        src_ref=src,
        dst_ref=dst,
        send_sem=send_sem,
        recv_sem=recv_sem,
        device_id=where,
        device_id_type=pl.DeviceIdType.MESH,
    )


def wait_all(like, sem):
    pltpu.make_async_copy(like, like, sem).wait()


def tile_neighbours():
    district = lax.axis_index("district")
    tile = lax.axis_index("tile")
    tiles = lax.axis_size("tile")
    below = (district, lax.rem(tile + tiles - 1, tiles))
    above = (district, lax.rem(tile + 1, tiles))
    has_below = tile > 0
    has_above = tile < tiles - 1
    return below, above, has_below, has_above


def sort_pairs(keys, table, row):
    p = lax.broadcasted_iota(jnp.int32, (PAIRS, PAIRS), 0)
    q = lax.broadcasted_iota(jnp.int32, (PAIRS, PAIRS), 1)
    column = jnp.sum(jnp.where(p == q, keys, 0), axis=1, keepdims=True)
    ahead = jnp.logical_or(keys < column, jnp.logical_and(keys == column, q < p))
    rank = jnp.sum(jnp.where(ahead, 1, 0), axis=1, keepdims=True)
    table[row : row + 1, 0:PAIRS] = jnp.sum(jnp.where(rank == q, p, 0), axis=0, keepdims=True)
    lane = lax.broadcasted_iota(jnp.int32, (PAIRS, ROW), 1)
    table[row + 1 : row + 2, :] = jnp.sum(jnp.where(column <= lane, 1, 0), axis=0, keepdims=True)
    table[row + 2 : row + 3, :] = jnp.sum(jnp.where(column < lane, 1, 0), axis=0, keepdims=True)


def build_picks(rmap, count, picks):
    rows = lax.broadcasted_iota(jnp.int32, (ROW, ROW), 0)

    def block(o, carry):
        maps = rmap[0, pl.ds(pl.multiple_of(o * PB, PB), PB), :] + jnp.where(o < count, 0, 2 * ROW)
        for j in range(PB):
            picks[o * PB + j] = jnp.where(rows == maps[j : j + 1, :], 1.0, 0.0).astype(BF16)
        return carry

    lax.fori_loop(0, NB, block, 0)


def scatter_columns(rmap, count, grads, h):
    lane = lax.broadcasted_iota(jnp.int32, (ROW, ROW), 1)
    pair = lax.broadcasted_iota(jnp.int32, (PAIRS, ROW), 0)
    columns = jnp.transpose(rmap[0] + jnp.where(pair < count * PB, 0, 2 * ROW))
    for p in range(PAIRS):
        picks = jnp.where(columns[:, p : p + 1] == lane, 1.0, 0.0).astype(BF16)
        h[p] = jnp.dot(grads[p // PB], picks, preferred_element_type=F32).astype(BF16)


def scatter_grads(picks, gt, ht):
    def step(i, carry):
        for j in range(UNROLL):
            product = jnp.dot(picks[i * UNROLL + j], gt[i * (UNROLL // PB) + j // PB], preferred_element_type=F32)
            ht[i * UNROLL + j] = product.astype(BF16)
        return carry

    lax.fori_loop(0, PAIRS // UNROLL, step, 0)


def gather_rows(picks, pin, ext, gathered):
    def step(i, carry):
        for j in range(UNROLL):
            p = i * UNROLL + j
            gathered[p] = jnp.dot(ext[pin[0, p]], picks[p], preferred_element_type=F32).astype(BF16)
        return carry

    lax.fori_loop(0, PAIRS // UNROLL, step, 0)


def running_sums(product, row, keys, table, sums):
    def step(i, carry):
        total, before = carry
        for j in range(UNROLL):
            at = i * UNROLL + j
            p = table[row, at]
            key = keys[0, p]
            total = total * jnp.where(key == before, 1.0, 0.0) + product(p)
            sums[at] = total
            before = key
        return total, before

    lax.fori_loop(0, PAIRS // UNROLL, step, (jnp.zeros((C, ROW), F32), jnp.int32(-1)))


def sum_of(key, row, table, sums):
    upto = table[row + 1, key]
    some = jnp.where(upto > table[row + 2, key], 1.0, 0.0)
    return sums[jnp.maximum(upto - 1, 0)] * some


def pack(table, sums, packed):
    lane = lax.broadcasted_iota(jnp.int32, (C, ROW), 1)

    for q in range(7):
        a = sum_of(4 * q, 0, table, sums)
        b = pltpu.roll(sum_of(4 * q + 1, 0, table, sums), 96, 1)
        c = pltpu.roll(sum_of(4 * q + 2, 0, table, sums), 64, 1)
        d = pltpu.roll(sum_of(4 * q + 3, 0, table, sums), 32, 1)
        base = q * 3 * C
        packed[pl.ds(base, C), :] = jnp.where(lane < 96, a, b)
        packed[pl.ds(base + C, C), :] = jnp.where(lane < 64, b, c)
        packed[pl.ds(base + 2 * C, C), :] = jnp.where(lane < 32, c, d)
    packed[21 * C :, :] = jnp.zeros((PACKED - 21 * C, ROW), F32)


def fused_kernel(ny, nz, nx, *refs):
    (feat_in, pre_in, og_in, w1_in, w2_in, count_in, pin_in, poff_in, rmap_in, slo_in, shi_in,
     g1_ref, g2_ref, fg_ref,
     feat, pre, og, w1, w2, rmap, pin_v, poff_v, count, pin, poff, slo, shi, table_v, table,
     picks, gt, ht, gathered, sums, ext_h, ext_x, own,
     out_lo, out_hi, in_lo, in_hi, gb_lo, gb_hi, fb_lo, fb_hi, gb2_lo, gb2_hi, fb2_lo, fb2_hi,
     dwp, rcv0, snd1, rcv1, mine, gat3, fin1,
     load, tsem, hs, hr, gs, gr, g2s, g2r, s0, r0, s1, r1, s3, r3, s5, r5, s6, r6) = refs
    half = PACKED // 2
    district = lax.axis_index("district")
    tile = lax.axis_index("tile")
    core = lax.rem(district, 2)
    y = lax.div(district, 2)
    z = lax.div(tile, nx)
    x = lax.rem(tile, nx)
    below, above, has_below, has_above = tile_neighbours()
    other = (district + 1 - 2 * core, tile)

    def plane_of(n, me, device):
        steps = sorted(
            [(a, b) for a in range(n) for b in range(nx) if a + b],
            key=lambda step: -min(step[0], n - step[0]) - min(step[1], nx - step[1]),
        )
        places = [(lax.rem(me + a, n), lax.rem(x + b, nx)) for a, b in steps]
        return [i * nx + j for i, j in places], [device(i, j) for i, j in places]

    def line_of(n, me, device):
        order = sorted(range(1, n), key=lambda a: -min(a, n - a))
        return [device(lax.rem(me + a, n), x) for a in order]

    def over_y(i, j):
        return (i * 2 + core, z * nx + j)

    def over_z(i, j):
        return (district, i * nx + j)

    planes = (plane_of(ny, y, over_y), plane_of(nz, z, over_z))
    lines = (line_of(nz, z, over_z), line_of(ny, y, over_y))
    own_part = (y * nx + x, z * nx + x)
    own_slot = (z, y)
    parts = (half // (ny * nx), half // (nz * nx))
    slots = (nz, ny)

    loads = {}
    pieces = (("rmap", rmap_in, rmap), ("count", count_in, count), ("poff_v", poff_in, poff_v), ("pin_v", pin_in, pin_v),
              ("og", og_in, og), ("pin", pin_in, pin), ("poff", poff_in, poff), ("slo", slo_in, slo), ("shi", shi_in, shi),
              ("pre", pre_in, pre), ("feat", feat_in, feat), ("w2", w2_in, w2), ("w1", w1_in, w1))
    for i, (name, src, dst) in enumerate(pieces):
        loads[name] = pltpu.make_async_copy(src, dst, load.at[i])
        loads[name].start()
    barrier = pltpu.get_barrier_semaphore()
    peers = planes[0][1] + [other, below, above]
    peers += [over_z(lax.rem(z + a, nz), lax.rem(x + b, nx)) for a in range(1, nz) for b in range(nx)]
    for peer in peers:
        pl.semaphore_signal(barrier, inc=1, device_id=peer, device_id_type=pl.DeviceIdType.MESH)

    gt[...] = jnp.zeros_like(gt)
    table_v[...] = jnp.zeros_like(table_v)
    loads["poff_v"].wait()
    loads["pin_v"].wait()
    sort_pairs(poff_v[...], table_v, 0)
    sort_pairs(pin_v[...], table_v, 3)
    to_scalar = pltpu.make_async_copy(table_v, table, tsem)
    to_scalar.start()
    loads["rmap"].wait()
    loads["count"].wait()
    loads["og"].wait()
    scatter_columns(rmap, count[0, 0], og, gathered)

    for name in ("slo", "shi", "pre", "feat"):
        loads[name].wait()
    for j in range(KB):
        out_lo[0, j] = jnp.maximum(pre[slo[0, j]], 0.0)
        out_hi[0, j] = jnp.maximum(pre[shi[0, j]], 0.0)
        out_lo[1, j] = feat[slo[0, j]]
        out_hi[1, j] = feat[shi[0, j]]
    pl.semaphore_wait(barrier, len(peers))
    halo = []
    for f in range(2):
        halo.append((
            remote(out_hi.at[f], in_lo.at[f], hs.at[0, f], hr.at[0, f], above),
            remote(out_lo.at[f], in_hi.at[f], hs.at[1, f], hr.at[1, f], below),
        ))
    for copy in list(halo[0]) + list(halo[1]):
        copy.start()

    for name in ("pin", "poff", "w2"):
        loads[name].wait()
    to_scalar.wait()
    running_sums(
        lambda p: jnp.dot(w2[poff[0, p]], gathered[p], preferred_element_type=F32),
        3, pin, table, sums,
    )
    for j in range(KB):
        gb_lo[j] = sum_of(NB + j, 3, table, sums).astype(gb_lo.dtype)
        gb_hi[j] = sum_of(NB + KB + j, 3, table, sums).astype(gb_hi.dtype)
    for b in range(NB):
        own[b] = sum_of(b, 3, table, sums)
    back = (
        remote(gb_hi, fb_lo, gs.at[0], gr.at[0], above),
        remote(gb_lo, fb_hi, gs.at[1], gr.at[1], below),
    )
    for copy in back:
        copy.start()

    build_picks(rmap, count[0, 0], picks)
    for b in range(NB):
        gt[b, :, 0:C] = jnp.transpose(og[b])
    scatter_grads(picks, gt, ht)

    def extend(f, own, ext):
        ext[0:NB] = own
        halo[f][0].wait()
        ext[NB : NB + KB] = jnp.where(has_below, in_lo[f], jnp.zeros_like(in_lo[f]))
        halo[f][1].wait()
        ext[NB + KB :] = jnp.where(has_above, in_hi[f], jnp.zeros_like(in_hi[f]))

    keep = pl.ds(pl.multiple_of(core * half, half), half)
    away = pl.ds(pl.multiple_of((1 - core) * half, half), half)
    chunks = [pl.ds(pl.multiple_of(own_part[g] * parts[g], parts[g]), parts[g]) for g in range(2)]
    outs = (g1_ref, g2_ref)

    def swap_halves(g):
        remote(dwp.at[g, away, :], rcv0.at[g], s0.at[g], r0.at[g], other).start()

    def scatter_plane(g):
        wait_all(rcv0.at[g], r0.at[g])
        snd1[g] = (dwp[g, keep, :] + rcv0[g]).astype(BF16)
        part = parts[g]
        for s, (index, peer) in enumerate(zip(*planes[g])):
            rows = pl.ds(pl.multiple_of(index * part, part), part)
            remote(snd1.at[g, rows, :], rcv1.at[g, s, 0:part], s1.at[g], r1.at[g], peer).start()
        at = pl.ds(pl.multiple_of(core * half + own_part[g] * part, part), part)
        mine[g, 0:part] = dwp[g, at, :] + rcv0[g, chunks[g], :]

    def exchange_line(g):
        part = parts[g]
        near = half // part - 1
        wait_all(rcv1.at[g, 0:near, 0:part], r1.at[g])
        total = mine[g, 0:part]
        for s in range(near):
            total = total + rcv1[g, s, 0:part].astype(F32)
        gat3[g, own_slot[g], 0:part] = total.astype(BF16)
        for peer in lines[g]:
            block = gat3.at[g, own_slot[g], 0:part]
            remote(block, block, s3.at[g], r3.at[g], peer).start()

    def gather_plane(g):
        part = parts[g]
        wait_all(gat3.at[g, 0 : slots[g] - 1, 0:part], r3.at[g])
        total = gat3[g, 0, 0:part].astype(F32)
        for i in range(1, slots[g]):
            total = total + gat3[g, i, 0:part].astype(F32)
        fin1[g, chunks[g], :] = total.astype(BF16)
        block = fin1.at[g, chunks[g], :]
        for peer in planes[g][1]:
            remote(block, block, s5.at[g], r5.at[g], peer).start()

    def share_halves(g):
        wait_all(fin1.at[g, 0 : half - parts[g]], r5.at[g])
        remote(fin1.at[g], outs[g].at[keep, :], s6.at[g], r6.at[g], other).start()
        outs[g][keep, :] = fin1[g]

    def settle(g):
        wait_all(rcv0.at[g], s0.at[g])
        wait_all(snd1.at[g, 0 : half - parts[g]], s1.at[g])
        wait_all(gat3.at[g, 0 : slots[g] - 1, 0 : parts[g]], s3.at[g])
        wait_all(fin1.at[g, 0 : half - parts[g]], s5.at[g])
        wait_all(fin1.at[g], s6.at[g])
        wait_all(fin1.at[g], r6.at[g])

    def add_back(b, total, lo, hi):
        for j in range(KB):
            from_below = jnp.where(jnp.logical_and(slo[0, j] == b, has_below), 1.0, 0.0)
            from_above = jnp.where(jnp.logical_and(shi[0, j] == b, has_above), 1.0, 0.0)
            total = total + from_below * lo[j].astype(F32) + from_above * hi[j].astype(F32)
        return total

    extend(0, jnp.maximum(pre[...], 0.0), ext_h)
    running_sums(
        lambda p: jnp.dot(ext_h[pin[0, p]], ht[p], preferred_element_type=F32), 0, poff, table, sums
    )
    pack(table, sums, dwp.at[1])
    swap_halves(1)
    extend(1, feat[...], ext_x)
    gather_rows(picks, pin, ext_x, gathered)
    for copy in back:
        copy.wait()
    for b in range(NB):
        hidden_grad = add_back(b, own[b], fb_lo, fb_hi)
        gt[b, :, 0:C] = jnp.transpose(jnp.where(pre[b] > 0, hidden_grad, 0.0).astype(BF16))
    running_sums(
        lambda p: jnp.dot(gathered[p], gt[p // PB], preferred_element_type=F32), 0, poff, table, sums
    )
    pack(table, sums, dwp.at[0])
    swap_halves(0)

    scatter_plane(1)
    scatter_plane(0)

    scatter_grads(picks, gt, ht)
    loads["w1"].wait()
    running_sums(
        lambda p: lax.dot_general(w1[poff[0, p]], ht[p, :, 0:C], NT, preferred_element_type=F32),
        3, pin, table, sums,
    )
    for j in range(KB):
        gb2_lo[j] = sum_of(NB + j, 3, table, sums)
        gb2_hi[j] = sum_of(NB + KB + j, 3, table, sums)
    for b in range(NB):
        own[b] = sum_of(b, 3, table, sums)

    exchange_line(1)
    exchange_line(0)
    last = (
        remote(gb2_hi, fb2_lo, g2s.at[0], g2r.at[0], above),
        remote(gb2_lo, fb2_hi, g2s.at[1], g2r.at[1], below),
    )
    for copy in last:
        copy.start()
    gather_plane(1)
    gather_plane(0)
    for copy in last:
        copy.wait()
    for b in range(NB):
        fg_ref[b] = add_back(b, own[b], fb2_lo, fb2_hi).astype(BF16)
    share_halves(1)
    share_halves(0)
    settle(0)
    settle(1)


def fused(ny, nz, nx, *operands):
    half = PACKED // 2
    part = half // (min(ny, nz) * nx)
    most = max(ny, nz)
    near = most * nx - 1
    dma = pltpu.SemaphoreType.DMA
    packed = jax.ShapeDtypeStruct((PACKED, ROW), BF16)
    blocks = jax.ShapeDtypeStruct((NB, C, ROW), BF16)
    four = pltpu.VMEM((NB, C, ROW), BF16)
    four_wide = pltpu.VMEM((NB, C, ROW), F32)
    kernel_weights = pltpu.VMEM((K, C, C), BF16)
    return pl.pallas_call(
        functools.partial(fused_kernel, ny, nz, nx),
        out_shape=(packed, packed, blocks),
        in_specs=[HBM] * 11,
        out_specs=(VMEM,) * 3,
        scratch_shapes=[
            four, four, four, kernel_weights, kernel_weights,
            pltpu.VMEM((1, PAIRS, ROW), jnp.int32),
            pltpu.VMEM((1, PAIRS), jnp.int32),
            pltpu.VMEM((1, PAIRS), jnp.int32),
            pltpu.SMEM((1, 1), jnp.int32),
            pltpu.SMEM((1, PAIRS), jnp.int32),
            pltpu.SMEM((1, PAIRS), jnp.int32),
            pltpu.SMEM((1, KB), jnp.int32),
            pltpu.SMEM((1, KB), jnp.int32),
            pltpu.VMEM((8, ROW), jnp.int32),
            pltpu.SMEM((8, ROW), jnp.int32),
            pltpu.VMEM((PAIRS, ROW, ROW), BF16),
            pltpu.VMEM((NB, ROW, ROW), BF16),
            pltpu.VMEM((PAIRS, ROW, ROW), BF16),
            pltpu.VMEM((PAIRS, C, ROW), BF16),
            pltpu.VMEM((PAIRS, C, ROW), F32),
            pltpu.VMEM((EXT, C, ROW), BF16),
            pltpu.VMEM((EXT, C, ROW), BF16),
            four_wide,
            pltpu.VMEM((2, KB, C, ROW), BF16),
            pltpu.VMEM((2, KB, C, ROW), BF16),
            pltpu.VMEM((2, KB, C, ROW), BF16),
            pltpu.VMEM((2, KB, C, ROW), BF16),
            four, four, four, four, four_wide, four_wide, four_wide, four_wide,
            pltpu.VMEM((2, PACKED, ROW), F32),
            pltpu.VMEM((2, half, ROW), F32),
            pltpu.VMEM((2, half, ROW), BF16),
            pltpu.VMEM((2, near, part, ROW), BF16),
            pltpu.VMEM((2, part, ROW), F32),
            pltpu.VMEM((2, most, part, ROW), BF16),
            pltpu.VMEM((2, half, ROW), BF16),
            dma((13,)), dma,
            dma((2, 2)), dma((2, 2)),
            dma((2,)), dma((2,)),
            dma((2,)), dma((2,)),
            dma((2,)), dma((2,)),
            dma((2,)), dma((2,)),
            dma((2,)), dma((2,)),
            dma((2,)), dma((2,)),
            dma((2,)), dma((2,)),
        ],
        compiler_params=pltpu.CompilerParams(
            collective_id=0, has_side_effects=True, vmem_limit_bytes=VMEM_LIMIT
        ),
        name="fused",
    )(*operands)


def finish_kernel(grad_ref, g1_ref, g2_ref, fg_ref, w1_ref, w2_ref, wide, sems, last):
    lane = lax.broadcasted_iota(jnp.int32, (C, ROW), 1)
    first = pltpu.make_async_copy(grad_ref, fg_ref, last)
    first.start()
    copies = [first]
    for g, (src, dst) in enumerate(((g1_ref, w1_ref), (g2_ref, w2_ref))):
        for q in range(7):
            base = q * 3 * C
            size = min(4, K - 4 * q)
            r1 = src[base : base + C, :].astype(F32)
            r2 = src[base + C : base + 2 * C, :].astype(F32)
            r3 = src[base + 2 * C : base + 3 * C, :].astype(F32)
            wide[g, 4 * q] = r1[:, 0:C]
            wide[g, 4 * q + 1] = pltpu.roll(jnp.where(lane < 96, r2, r1), 32, 1)[:, 0:C]
            wide[g, 4 * q + 2] = pltpu.roll(jnp.where(lane < 64, r3, r2), 64, 1)[:, 0:C]
            if size == 4:
                wide[g, 4 * q + 3] = pltpu.roll(r3, 96, 1)[:, 0:C]
            copy = pltpu.make_async_copy(
                wide.at[g, pl.ds(4 * q, size)], dst.at[pl.ds(4 * q, size)], sems.at[g, q]
            )
            copy.start()
            copies.append(copy)
    for copy in copies:
        copy.wait()


def finish(grad, g1, g2):
    kern = jax.ShapeDtypeStruct((K, C, C), F32)
    return pl.pallas_call(
        finish_kernel,
        out_shape=(jax.ShapeDtypeStruct((NB, C, ROW), BF16), kern, kern),
        in_specs=[VMEM] * 3,
        out_specs=(HBM,) * 3,
        scratch_shapes=[
            pltpu.VMEM((2, K, C, C), F32),
            pltpu.SemaphoreType.DMA((2, 7)),
            pltpu.SemaphoreType.DMA,
        ],
        compiler_params=pltpu.CompilerParams(vmem_limit_bytes=VMEM_LIMIT),
        name="finish",
    )(grad, g1, g2)


def body(ny, nz, nx, features, pre_act, out_grad, weight_one, weight_two, block_count, pair_in, pair_off,
         row_map, send_lo, send_hi):
    operands = (features, pre_act, out_grad, weight_one, weight_two, block_count.reshape(1, 1), pair_in, pair_off,
                row_map, send_lo, send_hi)
    operands = [a if a.size == 1 else pltpu.with_memory_space_constraint(a, pltpu.HBM) for a in operands]
    g1, g2, grad = fused(ny, nz, nx, *operands)
    return finish(grad, g1, g2)


def solution(mesh):
    placed = (
        P(("district", "tile"), None, None),
        P(("district", "tile"), None, None),
        P(("district", "tile"), None, None),
        P(),
        P(),
        P(("district", "tile")),
        P(("district", "tile"), None),
        P(("district", "tile"), None),
        P(("district", "tile"), None, None),
        P(("district", "tile"), None),
        P(("district", "tile"), None),
    )
    tiles = mesh.shape["tile"]
    nx = 4 if tiles % 4 == 0 and tiles > 4 else 2
    ny, nz = mesh.shape["district"] // 2, tiles // nx
    return jax.shard_map(
        functools.partial(body, ny, nz, nx),
        mesh=mesh,
        in_specs=placed,
        out_specs=(P(("district", "tile"), None, None), P(), P()),
        check_vma=False,
    )
```

```python
import functools

import jax
import jax.numpy as jnp
from jax import lax
from jax.experimental import pallas as pl
from jax.experimental.pallas import tpu as pltpu
from jax.sharding import PartitionSpec as P

K = 27
PB = 16
NB = 4
KB = 4
C = 96
ROW = 128
EXT = NB + 2 * KB
PAIRS = NB * PB
UNROLL = 64
NT = (((1,), (1,)), ((), ()))
PACKED = 2048
F32 = jnp.float32
BF16 = jnp.bfloat16
VMEM_LIMIT = 28 * 1024 * 1024

HBM = pl.BlockSpec(memory_space=pltpu.HBM)
VMEM = pl.BlockSpec(memory_space=pltpu.VMEM)


def remote(src, dst, send_sem, recv_sem, where):
    return pltpu.make_async_remote_copy(
        src_ref=src,
        dst_ref=dst,
        send_sem=send_sem,
        recv_sem=recv_sem,
        device_id=where,
        device_id_type=pl.DeviceIdType.MESH,
    )


def wait_all(like, sem):
    pltpu.make_async_copy(like, like, sem).wait()


def tile_neighbours():
    district = lax.axis_index("district")
    tile = lax.axis_index("tile")
    tiles = lax.axis_size("tile")
    below = (district, lax.rem(tile + tiles - 1, tiles))
    above = (district, lax.rem(tile + 1, tiles))
    has_below = tile > 0
    has_above = tile < tiles - 1
    return below, above, has_below, has_above


def sort_pairs(keys, table, row):
    p = lax.broadcasted_iota(jnp.int32, (PAIRS, PAIRS), 0)
    q = lax.broadcasted_iota(jnp.int32, (PAIRS, PAIRS), 1)
    column = jnp.sum(jnp.where(p == q, keys, 0), axis=1, keepdims=True)
    ahead = jnp.logical_or(keys < column, jnp.logical_and(keys == column, q < p))
    rank = jnp.sum(jnp.where(ahead, 1, 0), axis=1, keepdims=True)
    table[row : row + 1, 0:PAIRS] = jnp.sum(jnp.where(rank == q, p, 0), axis=0, keepdims=True)
    lane = lax.broadcasted_iota(jnp.int32, (PAIRS, ROW), 1)
    table[row + 1 : row + 2, :] = jnp.sum(jnp.where(column <= lane, 1, 0), axis=0, keepdims=True)
    table[row + 2 : row + 3, :] = jnp.sum(jnp.where(column < lane, 1, 0), axis=0, keepdims=True)


def build_picks(rmap, count, picks):
    rows = lax.broadcasted_iota(jnp.int32, (ROW, ROW), 0)

    def block(o, carry):
        maps = rmap[0, pl.ds(pl.multiple_of(o * PB, PB), PB), :] + jnp.where(o < count, 0, 2 * ROW)
        for j in range(PB):
            picks[o * PB + j] = jnp.where(rows == maps[j : j + 1, :], 1.0, 0.0).astype(BF16)
        return carry

    lax.fori_loop(0, NB, block, 0)


def scatter_columns(rmap, count, grads, h):
    lane = lax.broadcasted_iota(jnp.int32, (ROW, ROW), 1)
    pair = lax.broadcasted_iota(jnp.int32, (PAIRS, ROW), 0)
    columns = jnp.transpose(rmap[0] + jnp.where(pair < count * PB, 0, 2 * ROW))
    for p in range(PAIRS):
        picks = jnp.where(columns[:, p : p + 1] == lane, 1.0, 0.0).astype(BF16)
        h[p] = jnp.dot(grads[p // PB], picks, preferred_element_type=F32).astype(BF16)


def scatter_grads(picks, gt, ht):
    def step(i, carry):
        for j in range(UNROLL):
            product = jnp.dot(picks[i * UNROLL + j], gt[i * (UNROLL // PB) + j // PB], preferred_element_type=F32)
            ht[i * UNROLL + j] = product.astype(BF16)
        return carry

    lax.fori_loop(0, PAIRS // UNROLL, step, 0)


def gather_rows(picks, pin, ext, gathered):
    def step(i, carry):
        for j in range(UNROLL):
            p = i * UNROLL + j
            gathered[p] = jnp.dot(ext[pin[0, p]], picks[p], preferred_element_type=F32).astype(BF16)
        return carry

    lax.fori_loop(0, PAIRS // UNROLL, step, 0)


def running_sums(product, row, keys, table, sums):
    def step(i, carry):
        total, before = carry
        for j in range(UNROLL):
            at = i * UNROLL + j
            p = table[row, at]
            key = keys[0, p]
            total = total * jnp.where(key == before, 1.0, 0.0) + product(p)
            sums[at] = total
            before = key
        return total, before

    lax.fori_loop(0, PAIRS // UNROLL, step, (jnp.zeros((C, ROW), F32), jnp.int32(-1)))


def sum_of(key, row, table, sums):
    upto = table[row + 1, key]
    some = jnp.where(upto > table[row + 2, key], 1.0, 0.0)
    return sums[jnp.maximum(upto - 1, 0)] * some


def pack(table, sums, packed):
    lane = lax.broadcasted_iota(jnp.int32, (C, ROW), 1)

    for q in range(7):
        a = sum_of(4 * q, 0, table, sums)
        b = pltpu.roll(sum_of(4 * q + 1, 0, table, sums), 96, 1)
        c = pltpu.roll(sum_of(4 * q + 2, 0, table, sums), 64, 1)
        d = pltpu.roll(sum_of(4 * q + 3, 0, table, sums), 32, 1)
        base = q * 3 * C
        packed[pl.ds(base, C), :] = jnp.where(lane < 96, a, b)
        packed[pl.ds(base + C, C), :] = jnp.where(lane < 64, b, c)
        packed[pl.ds(base + 2 * C, C), :] = jnp.where(lane < 32, c, d)
    packed[21 * C :, :] = jnp.zeros((PACKED - 21 * C, ROW), F32)


def fused_kernel(ny, nz, nx, *refs):
    (feat_in, pre_in, og_in, w1_in, w2_in, count_in, pin_in, poff_in, rmap_in, slo_in, shi_in,
     g1_ref, g2_ref, fg_ref,
     feat, pre, og, w1, w2, rmap, pin_v, poff_v, count, pin, poff, slo, shi, table_v, table,
     picks, gt, ht, gathered, sums, ext_h, ext_x, own,
     out_lo, out_hi, in_lo, in_hi, gb_lo, gb_hi, fb_lo, fb_hi, gb2_lo, gb2_hi, fb2_lo, fb2_hi,
     dwp, rcv0, snd1, rcv1, mine, gat3, fin1,
     load, tsem, hs, hr, gs, gr, g2s, g2r, s0, r0, s1, r1, s3, r3, s5, r5, s6, r6) = refs
    half = PACKED // 2
    district = lax.axis_index("district")
    tile = lax.axis_index("tile")
    core = lax.rem(district, 2)
    y = lax.div(district, 2)
    z = lax.div(tile, nx)
    x = lax.rem(tile, nx)
    below, above, has_below, has_above = tile_neighbours()
    other = (district + 1 - 2 * core, tile)

    def across(flip, first, i, j):
        over_y = ((i * 2 + core), (z * nx + j))
        over_z = (district, (i * nx + j))
        along = 1 - flip if first else flip
        return tuple(a * along + b * (1 - along) for a, b in zip(over_y, over_z))

    def plane_of(flip):
        me = y * (1 - flip) + z * flip
        steps = sorted(
            [(a, b) for a in range(ny) for b in range(nx) if a + b],
            key=lambda step: -min(step[0], ny - step[0]) - min(step[1], nx - step[1]),
        )
        places = [(lax.rem(me + a, ny), lax.rem(x + b, nx)) for a, b in steps]
        return [i * nx + j for i, j in places], [across(flip, True, i, j) for i, j in places]

    def line_of(flip):
        me = y * flip + z * (1 - flip)
        order = sorted(range(1, nz), key=lambda a: -min(a, nz - a))
        return [across(flip, False, lax.rem(me + a, nz), x) for a in order]

    flips = (core, 1 - core)
    planes = [plane_of(flip) for flip in flips]
    lines = [line_of(flip) for flip in flips]
    own_part = [(y * (1 - flip) + z * flip) * nx + x for flip in flips]
    own_slot = [y * flip + z * (1 - flip) for flip in flips]
    parts = (half // (ny * nx),) * 2
    slots = (nz, nz)

    loads = {}
    pieces = (("rmap", rmap_in, rmap), ("count", count_in, count), ("poff_v", poff_in, poff_v), ("pin_v", pin_in, pin_v),
              ("og", og_in, og), ("pin", pin_in, pin), ("poff", poff_in, poff), ("slo", slo_in, slo), ("shi", shi_in, shi),
              ("pre", pre_in, pre), ("feat", feat_in, feat), ("w2", w2_in, w2), ("w1", w1_in, w1))
    for i, (name, src, dst) in enumerate(pieces):
        loads[name] = pltpu.make_async_copy(src, dst, load.at[i])
        loads[name].start()
    barrier = pltpu.get_barrier_semaphore()
    peers = planes[0][1] + planes[1][1] + [other, below, above]
    for peer in peers:
        pl.semaphore_signal(barrier, inc=1, device_id=peer, device_id_type=pl.DeviceIdType.MESH)

    gt[...] = jnp.zeros_like(gt)
    table_v[...] = jnp.zeros_like(table_v)
    loads["poff_v"].wait()
    loads["pin_v"].wait()
    sort_pairs(poff_v[...], table_v, 0)
    sort_pairs(pin_v[...], table_v, 3)
    to_scalar = pltpu.make_async_copy(table_v, table, tsem)
    to_scalar.start()
    loads["rmap"].wait()
    loads["count"].wait()
    loads["og"].wait()
    scatter_columns(rmap, count[0, 0], og, gathered)

    for name in ("slo", "shi", "pre", "feat"):
        loads[name].wait()
    for j in range(KB):
        out_lo[0, j] = jnp.maximum(pre[slo[0, j]], 0.0)
        out_hi[0, j] = jnp.maximum(pre[shi[0, j]], 0.0)
        out_lo[1, j] = feat[slo[0, j]]
        out_hi[1, j] = feat[shi[0, j]]
    for name in ("pin", "poff", "w2"):
        loads[name].wait()
    to_scalar.wait()
    running_sums(
        lambda p: jnp.dot(w2[poff[0, p]], gathered[p], preferred_element_type=F32),
        3, pin, table, sums,
    )
    for j in range(KB):
        gb_lo[j] = sum_of(NB + j, 3, table, sums).astype(gb_lo.dtype)
        gb_hi[j] = sum_of(NB + KB + j, 3, table, sums).astype(gb_hi.dtype)
    for b in range(NB):
        own[b] = sum_of(b, 3, table, sums)
    pl.semaphore_wait(barrier, len(peers))
    halo = []
    for f in range(2):
        halo.append((
            remote(out_hi.at[f], in_lo.at[f], hs.at[0, f], hr.at[0, f], above),
            remote(out_lo.at[f], in_hi.at[f], hs.at[1, f], hr.at[1, f], below),
        ))
    back = (
        remote(gb_hi, fb_lo, gs.at[0], gr.at[0], above),
        remote(gb_lo, fb_hi, gs.at[1], gr.at[1], below),
    )
    for copy in list(halo[1]) + list(back) + list(halo[0]):
        copy.start()

    build_picks(rmap, count[0, 0], picks)
    for b in range(NB):
        gt[b, :, 0:C] = jnp.transpose(og[b])
    scatter_grads(picks, gt, ht)

    def extend(f, own, ext):
        ext[0:NB] = own
        halo[f][0].wait()
        ext[NB : NB + KB] = jnp.where(has_below, in_lo[f], jnp.zeros_like(in_lo[f]))
        halo[f][1].wait()
        ext[NB + KB :] = jnp.where(has_above, in_hi[f], jnp.zeros_like(in_hi[f]))

    keep = pl.ds(pl.multiple_of(core * half, half), half)
    away = pl.ds(pl.multiple_of((1 - core) * half, half), half)
    chunks = [pl.ds(pl.multiple_of(own_part[g] * parts[g], parts[g]), parts[g]) for g in range(2)]
    outs = (g1_ref, g2_ref)

    def swap_halves(g):
        remote(dwp.at[g, away, :], rcv0.at[g], s0.at[g], r0.at[g], other).start()

    def scatter_plane(g):
        wait_all(rcv0.at[g], r0.at[g])
        snd1[g] = (dwp[g, keep, :] + rcv0[g]).astype(BF16)
        part = parts[g]
        for s, (index, peer) in enumerate(zip(*planes[g])):
            rows = pl.ds(pl.multiple_of(index * part, part), part)
            remote(snd1.at[g, rows, :], rcv1.at[g, s, 0:part], s1.at[g], r1.at[g], peer).start()
        at = pl.ds(pl.multiple_of(core * half + own_part[g] * part, part), part)
        mine[g, 0:part] = dwp[g, at, :] + rcv0[g, chunks[g], :]

    def exchange_line(g):
        part = parts[g]
        near = half // part - 1
        wait_all(rcv1.at[g, 0:near, 0:part], r1.at[g])
        total = mine[g, 0:part]
        for s in range(near):
            total = total + rcv1[g, s, 0:part].astype(F32)
        gat3[g, own_slot[g], 0:part] = total.astype(BF16)
        for peer in lines[g]:
            block = gat3.at[g, own_slot[g], 0:part]
            remote(block, block, s3.at[g], r3.at[g], peer).start()

    def gather_plane(g):
        part = parts[g]
        wait_all(gat3.at[g, 0 : slots[g] - 1, 0:part], r3.at[g])
        total = gat3[g, 0, 0:part].astype(F32)
        for i in range(1, slots[g]):
            total = total + gat3[g, i, 0:part].astype(F32)
        fin1[g, chunks[g], :] = total.astype(BF16)
        block = fin1.at[g, chunks[g], :]
        for peer in planes[g][1]:
            remote(block, block, s5.at[g], r5.at[g], peer).start()

    def share_halves(g):
        wait_all(fin1.at[g, 0 : half - parts[g]], r5.at[g])
        remote(fin1.at[g], outs[g].at[keep, :], s6.at[g], r6.at[g], other).start()
        outs[g][keep, :] = fin1[g]

    def settle(g):
        wait_all(rcv0.at[g], s0.at[g])
        wait_all(snd1.at[g, 0 : half - parts[g]], s1.at[g])
        wait_all(gat3.at[g, 0 : slots[g] - 1, 0 : parts[g]], s3.at[g])
        wait_all(fin1.at[g, 0 : half - parts[g]], s5.at[g])
        wait_all(fin1.at[g], s6.at[g])
        wait_all(fin1.at[g], r6.at[g])

    def add_back(b, total, lo, hi):
        for j in range(KB):
            from_below = jnp.where(jnp.logical_and(slo[0, j] == b, has_below), 1.0, 0.0)
            from_above = jnp.where(jnp.logical_and(shi[0, j] == b, has_above), 1.0, 0.0)
            total = total + from_below * lo[j].astype(F32) + from_above * hi[j].astype(F32)
        return total

    extend(1, feat[...], ext_x)
    gather_rows(picks, pin, ext_x, gathered)
    for copy in back:
        copy.wait()
    for b in range(NB):
        hidden_grad = add_back(b, own[b], fb_lo, fb_hi)
        gt[b, :, 0:C] = jnp.transpose(jnp.where(pre[b] > 0, hidden_grad, 0.0).astype(BF16))
    running_sums(
        lambda p: jnp.dot(gathered[p], gt[p // PB], preferred_element_type=F32), 0, poff, table, sums
    )
    pack(table, sums, dwp.at[0])
    swap_halves(0)

    extend(0, jnp.maximum(pre[...], 0.0), ext_h)
    running_sums(
        lambda p: jnp.dot(ext_h[pin[0, p]], ht[p], preferred_element_type=F32), 0, poff, table, sums
    )
    pack(table, sums, dwp.at[1])
    swap_halves(1)
    scatter_plane(0)
    scatter_plane(1)

    scatter_grads(picks, gt, ht)
    loads["w1"].wait()
    running_sums(
        lambda p: lax.dot_general(w1[poff[0, p]], ht[p, :, 0:C], NT, preferred_element_type=F32),
        3, pin, table, sums,
    )
    for j in range(KB):
        gb2_lo[j] = sum_of(NB + j, 3, table, sums)
        gb2_hi[j] = sum_of(NB + KB + j, 3, table, sums)
    for b in range(NB):
        own[b] = sum_of(b, 3, table, sums)

    exchange_line(0)
    exchange_line(1)
    last = (
        remote(gb2_hi, fb2_lo, g2s.at[0], g2r.at[0], above),
        remote(gb2_lo, fb2_hi, g2s.at[1], g2r.at[1], below),
    )
    for copy in last:
        copy.start()
    gather_plane(0)
    gather_plane(1)
    for copy in last:
        copy.wait()
    for b in range(NB):
        fg_ref[b] = add_back(b, own[b], fb2_lo, fb2_hi).astype(BF16)
    share_halves(0)
    share_halves(1)
    settle(0)
    settle(1)


def fused(ny, nz, nx, *operands):
    half = PACKED // 2
    part = half // (min(ny, nz) * nx)
    most = max(ny, nz)
    near = most * nx - 1
    dma = pltpu.SemaphoreType.DMA
    packed = jax.ShapeDtypeStruct((PACKED, ROW), BF16)
    blocks = jax.ShapeDtypeStruct((NB, C, ROW), BF16)
    four = pltpu.VMEM((NB, C, ROW), BF16)
    four_wide = pltpu.VMEM((NB, C, ROW), F32)
    kernel_weights = pltpu.VMEM((K, C, C), BF16)
    return pl.pallas_call(
        functools.partial(fused_kernel, ny, nz, nx),
        out_shape=(packed, packed, blocks),
        in_specs=[HBM] * 11,
        out_specs=(VMEM,) * 3,
        scratch_shapes=[
            four, four, four, kernel_weights, kernel_weights,
            pltpu.VMEM((1, PAIRS, ROW), jnp.int32),
            pltpu.VMEM((1, PAIRS), jnp.int32),
            pltpu.VMEM((1, PAIRS), jnp.int32),
            pltpu.SMEM((1, 1), jnp.int32),
            pltpu.SMEM((1, PAIRS), jnp.int32),
            pltpu.SMEM((1, PAIRS), jnp.int32),
            pltpu.SMEM((1, KB), jnp.int32),
            pltpu.SMEM((1, KB), jnp.int32),
            pltpu.VMEM((8, ROW), jnp.int32),
            pltpu.SMEM((8, ROW), jnp.int32),
            pltpu.VMEM((PAIRS, ROW, ROW), BF16),
            pltpu.VMEM((NB, ROW, ROW), BF16),
            pltpu.VMEM((PAIRS, ROW, ROW), BF16),
            pltpu.VMEM((PAIRS, C, ROW), BF16),
            pltpu.VMEM((PAIRS, C, ROW), F32),
            pltpu.VMEM((EXT, C, ROW), BF16),
            pltpu.VMEM((EXT, C, ROW), BF16),
            four_wide,
            pltpu.VMEM((2, KB, C, ROW), BF16),
            pltpu.VMEM((2, KB, C, ROW), BF16),
            pltpu.VMEM((2, KB, C, ROW), BF16),
            pltpu.VMEM((2, KB, C, ROW), BF16),
            four, four, four, four, four_wide, four_wide, four_wide, four_wide,
            pltpu.VMEM((2, PACKED, ROW), F32),
            pltpu.VMEM((2, half, ROW), F32),
            pltpu.VMEM((2, half, ROW), BF16),
            pltpu.VMEM((2, near, part, ROW), BF16),
            pltpu.VMEM((2, part, ROW), F32),
            pltpu.VMEM((2, most, part, ROW), BF16),
            pltpu.VMEM((2, half, ROW), BF16),
            dma((13,)), dma,
            dma((2, 2)), dma((2, 2)),
            dma((2,)), dma((2,)),
            dma((2,)), dma((2,)),
            dma((2,)), dma((2,)),
            dma((2,)), dma((2,)),
            dma((2,)), dma((2,)),
            dma((2,)), dma((2,)),
            dma((2,)), dma((2,)),
        ],
        compiler_params=pltpu.CompilerParams(
            collective_id=0, has_side_effects=True, vmem_limit_bytes=VMEM_LIMIT
        ),
        name="fused",
    )(*operands)


def finish_kernel(grad_ref, g1_ref, g2_ref, fg_ref, w1_ref, w2_ref, wide, sems, last):
    lane = lax.broadcasted_iota(jnp.int32, (C, ROW), 1)
    first = pltpu.make_async_copy(grad_ref, fg_ref, last)
    first.start()
    copies = [first]
    for g, (src, dst) in enumerate(((g1_ref, w1_ref), (g2_ref, w2_ref))):
        for q in range(7):
            base = q * 3 * C
            size = min(4, K - 4 * q)
            r1 = src[base : base + C, :].astype(F32)
            r2 = src[base + C : base + 2 * C, :].astype(F32)
            r3 = src[base + 2 * C : base + 3 * C, :].astype(F32)
            wide[g, 4 * q] = r1[:, 0:C]
            wide[g, 4 * q + 1] = pltpu.roll(jnp.where(lane < 96, r2, r1), 32, 1)[:, 0:C]
            wide[g, 4 * q + 2] = pltpu.roll(jnp.where(lane < 64, r3, r2), 64, 1)[:, 0:C]
            if size == 4:
                wide[g, 4 * q + 3] = pltpu.roll(r3, 96, 1)[:, 0:C]
            copy = pltpu.make_async_copy(
                wide.at[g, pl.ds(4 * q, size)], dst.at[pl.ds(4 * q, size)], sems.at[g, q]
            )
            copy.start()
            copies.append(copy)
    for copy in copies:
        copy.wait()


def finish(grad, g1, g2):
    kern = jax.ShapeDtypeStruct((K, C, C), F32)
    return pl.pallas_call(
        finish_kernel,
        out_shape=(jax.ShapeDtypeStruct((NB, C, ROW), BF16), kern, kern),
        in_specs=[VMEM] * 3,
        out_specs=(HBM,) * 3,
        scratch_shapes=[
            pltpu.VMEM((2, K, C, C), F32),
            pltpu.SemaphoreType.DMA((2, 7)),
            pltpu.SemaphoreType.DMA,
        ],
        compiler_params=pltpu.CompilerParams(vmem_limit_bytes=VMEM_LIMIT),
        name="finish",
    )(grad, g1, g2)


def body(ny, nz, nx, features, pre_act, out_grad, weight_one, weight_two, block_count, pair_in, pair_off,
         row_map, send_lo, send_hi):
    operands = (features, pre_act, out_grad, weight_one, weight_two, block_count.reshape(1, 1), pair_in, pair_off,
                row_map, send_lo, send_hi)
    operands = [a if a.size == 1 else pltpu.with_memory_space_constraint(a, pltpu.HBM) for a in operands]
    g1, g2, grad = fused(ny, nz, nx, *operands)
    return finish(grad, g1, g2)


def solution(mesh):
    placed = (
        P(("district", "tile"), None, None),
        P(("district", "tile"), None, None),
        P(("district", "tile"), None, None),
        P(),
        P(),
        P(("district", "tile")),
        P(("district", "tile"), None),
        P(("district", "tile"), None),
        P(("district", "tile"), None, None),
        P(("district", "tile"), None),
        P(("district", "tile"), None),
    )
    tiles = mesh.shape["tile"]
    nx = 4 if tiles % 4 == 0 and tiles > 4 else 2
    ny, nz = mesh.shape["district"] // 2, tiles // nx
    return jax.shard_map(
        functools.partial(body, ny, nz, nx),
        mesh=mesh,
        in_specs=placed,
        out_specs=(P(("district", "tile"), None, None), P(), P()),
        check_vma=False,
    )
```

```python
import functools

import jax
import jax.numpy as jnp
from jax import lax
from jax.experimental import pallas as pl
from jax.experimental.pallas import tpu as pltpu
from jax.sharding import PartitionSpec as P

K = 27
PB = 16
NB = 4
KB = 4
C = 96
ROW = 128
EXT = NB + 2 * KB
PAIRS = NB * PB
UNROLL = 64
NT = (((1,), (1,)), ((), ()))
PACKED = 2048
F32 = jnp.float32
BF16 = jnp.bfloat16
VMEM_LIMIT = 28 * 1024 * 1024

HBM = pl.BlockSpec(memory_space=pltpu.HBM)
VMEM = pl.BlockSpec(memory_space=pltpu.VMEM)


def remote(src, dst, send_sem, recv_sem, where):
    return pltpu.make_async_remote_copy(
        src_ref=src,
        dst_ref=dst,
        send_sem=send_sem,
        recv_sem=recv_sem,
        device_id=where,
        device_id_type=pl.DeviceIdType.MESH,
    )


def wait_all(like, sem):
    pltpu.make_async_copy(like, like, sem).wait()


def tile_neighbours():
    district = lax.axis_index("district")
    tile = lax.axis_index("tile")
    tiles = lax.axis_size("tile")
    below = (district, lax.rem(tile + tiles - 1, tiles))
    above = (district, lax.rem(tile + 1, tiles))
    has_below = tile > 0
    has_above = tile < tiles - 1
    return below, above, has_below, has_above


def sort_pairs(keys, table, row):
    p = lax.broadcasted_iota(jnp.int32, (PAIRS, PAIRS), 0)
    q = lax.broadcasted_iota(jnp.int32, (PAIRS, PAIRS), 1)
    column = jnp.sum(jnp.where(p == q, keys, 0), axis=1, keepdims=True)
    ahead = jnp.logical_or(keys < column, jnp.logical_and(keys == column, q < p))
    rank = jnp.sum(jnp.where(ahead, 1, 0), axis=1, keepdims=True)
    table[row : row + 1, 0:PAIRS] = jnp.sum(jnp.where(rank == q, p, 0), axis=0, keepdims=True)
    lane = lax.broadcasted_iota(jnp.int32, (PAIRS, ROW), 1)
    table[row + 1 : row + 2, :] = jnp.sum(jnp.where(column <= lane, 1, 0), axis=0, keepdims=True)
    table[row + 2 : row + 3, :] = jnp.sum(jnp.where(column < lane, 1, 0), axis=0, keepdims=True)


def build_picks(rmap, count, picks):
    rows = lax.broadcasted_iota(jnp.int32, (ROW, ROW), 0)

    def block(o, carry):
        maps = rmap[0, pl.ds(pl.multiple_of(o * PB, PB), PB), :] + jnp.where(o < count, 0, 2 * ROW)
        for j in range(PB):
            picks[o * PB + j] = jnp.where(rows == maps[j : j + 1, :], 1.0, 0.0).astype(BF16)
        return carry

    lax.fori_loop(0, NB, block, 0)


def scatter_columns(rmap, count, grads, h):
    lane = lax.broadcasted_iota(jnp.int32, (ROW, ROW), 1)
    pair = lax.broadcasted_iota(jnp.int32, (PAIRS, ROW), 0)
    columns = jnp.transpose(rmap[0] + jnp.where(pair < count * PB, 0, 2 * ROW))
    for p in range(PAIRS):
        picks = jnp.where(columns[:, p : p + 1] == lane, 1.0, 0.0).astype(BF16)
        h[p] = jnp.dot(grads[p // PB], picks, preferred_element_type=F32).astype(BF16)


def scatter_grads(picks, gt, ht):
    def step(i, carry):
        for j in range(UNROLL):
            product = jnp.dot(picks[i * UNROLL + j], gt[i * (UNROLL // PB) + j // PB], preferred_element_type=F32)
            ht[i * UNROLL + j] = product.astype(BF16)
        return carry

    lax.fori_loop(0, PAIRS // UNROLL, step, 0)


def gather_rows(picks, pin, ext, gathered):
    def step(i, carry):
        for j in range(UNROLL):
            p = i * UNROLL + j
            gathered[p] = jnp.dot(ext[pin[0, p]], picks[p], preferred_element_type=F32).astype(BF16)
        return carry

    lax.fori_loop(0, PAIRS // UNROLL, step, 0)


def running_sums(product, row, keys, table, sums):
    def step(i, carry):
        total, before = carry
        for j in range(UNROLL):
            at = i * UNROLL + j
            p = table[row, at]
            key = keys[0, p]
            total = total * jnp.where(key == before, 1.0, 0.0) + product(p)
            sums[at] = total
            before = key
        return total, before

    lax.fori_loop(0, PAIRS // UNROLL, step, (jnp.zeros((C, ROW), F32), jnp.int32(-1)))


def sum_of(key, row, table, sums):
    upto = table[row + 1, key]
    some = jnp.where(upto > table[row + 2, key], 1.0, 0.0)
    return sums[jnp.maximum(upto - 1, 0)] * some


def pack(table, sums, packed):
    lane = lax.broadcasted_iota(jnp.int32, (C, ROW), 1)

    for q in range(7):
        a = sum_of(4 * q, 0, table, sums)
        b = pltpu.roll(sum_of(4 * q + 1, 0, table, sums), 96, 1)
        c = pltpu.roll(sum_of(4 * q + 2, 0, table, sums), 64, 1)
        d = pltpu.roll(sum_of(4 * q + 3, 0, table, sums), 32, 1)
        base = q * 3 * C
        packed[pl.ds(base, C), :] = jnp.where(lane < 96, a, b)
        packed[pl.ds(base + C, C), :] = jnp.where(lane < 64, b, c)
        packed[pl.ds(base + 2 * C, C), :] = jnp.where(lane < 32, c, d)
    packed[21 * C :, :] = jnp.zeros((PACKED - 21 * C, ROW), F32)


def fused_kernel(ny, nz, nx, *refs):
    (feat_in, pre_in, og_in, w1_in, w2_in, count_in, pin_in, poff_in, rmap_in, slo_in, shi_in,
     g1_ref, g2_ref, fg_ref,
     feat, pre, og, w1, w2, rmap, pin_v, poff_v, count, pin, poff, slo, shi, table_v, table,
     picks, gt, ht, gathered, sums, ext_h, ext_x, own,
     out_lo, out_hi, in_lo, in_hi, gb_lo, gb_hi, fb_lo, fb_hi, gb2_lo, gb2_hi, fb2_lo, fb2_hi,
     dwp, snd0, rcv0, snd1, rcv1, mine, gat3, fin1,
     load, tsem, hs, hr, gs, gr, g2s, g2r, s0, r0, s1, r1, s3, r3, s5, r5, s6, r6) = refs
    half = PACKED // 2
    district = lax.axis_index("district")
    tile = lax.axis_index("tile")
    core = lax.rem(district, 2)
    y = lax.div(district, 2)
    z = lax.div(tile, nx)
    x = lax.rem(tile, nx)
    below, above, has_below, has_above = tile_neighbours()
    other = (district + 1 - 2 * core, tile)

    def plane_of(n, me, device):
        steps = sorted(
            [(a, b) for a in range(n) for b in range(nx) if a + b],
            key=lambda step: -min(step[0], n - step[0]) - min(step[1], nx - step[1]),
        )
        places = [(lax.rem(me + a, n), lax.rem(x + b, nx)) for a, b in steps]
        return [i * nx + j for i, j in places], [device(i, j) for i, j in places]

    def line_of(n, me, device):
        order = sorted(range(1, n), key=lambda a: -min(a, n - a))
        return [device(lax.rem(me + a, n), x) for a in order]

    def over_y(i, j):
        return (i * 2 + core, z * nx + j)

    def over_z(i, j):
        return (district, i * nx + j)

    planes = (plane_of(ny, y, over_y), plane_of(nz, z, over_z))
    lines = (line_of(nz, z, over_z), line_of(ny, y, over_y))
    own_part = (y * nx + x, z * nx + x)
    own_slot = (z, y)
    parts = (half // (ny * nx), half // (nz * nx))
    slots = (nz, ny)

    loads = {}
    pieces = (("rmap", rmap_in, rmap), ("count", count_in, count), ("poff_v", poff_in, poff_v), ("pin_v", pin_in, pin_v),
              ("og", og_in, og), ("pin", pin_in, pin), ("poff", poff_in, poff), ("slo", slo_in, slo), ("shi", shi_in, shi),
              ("pre", pre_in, pre), ("feat", feat_in, feat), ("w2", w2_in, w2), ("w1", w1_in, w1))
    for i, (name, src, dst) in enumerate(pieces):
        loads[name] = pltpu.make_async_copy(src, dst, load.at[i])
        loads[name].start()
    barrier = pltpu.get_barrier_semaphore()
    peers = planes[0][1] + [other, below, above]
    peers += [over_z(lax.rem(z + a, nz), lax.rem(x + b, nx)) for a in range(1, nz) for b in range(nx)]
    for peer in peers:
        pl.semaphore_signal(barrier, inc=1, device_id=peer, device_id_type=pl.DeviceIdType.MESH)

    gt[...] = jnp.zeros_like(gt)
    table_v[...] = jnp.zeros_like(table_v)
    loads["poff_v"].wait()
    loads["pin_v"].wait()
    sort_pairs(poff_v[...], table_v, 0)
    sort_pairs(pin_v[...], table_v, 3)
    to_scalar = pltpu.make_async_copy(table_v, table, tsem)
    to_scalar.start()
    loads["rmap"].wait()
    loads["count"].wait()
    loads["og"].wait()
    scatter_columns(rmap, count[0, 0], og, gathered)

    for name in ("slo", "shi", "pre", "feat"):
        loads[name].wait()
    for j in range(KB):
        out_lo[0, j] = jnp.maximum(pre[slo[0, j]], 0.0)
        out_hi[0, j] = jnp.maximum(pre[shi[0, j]], 0.0)
        out_lo[1, j] = feat[slo[0, j]]
        out_hi[1, j] = feat[shi[0, j]]
    for name in ("pin", "poff", "w2"):
        loads[name].wait()
    to_scalar.wait()
    running_sums(
        lambda p: jnp.dot(w2[poff[0, p]], gathered[p], preferred_element_type=F32),
        3, pin, table, sums,
    )
    for j in range(KB):
        gb_lo[j] = sum_of(NB + j, 3, table, sums).astype(gb_lo.dtype)
        gb_hi[j] = sum_of(NB + KB + j, 3, table, sums).astype(gb_hi.dtype)
    for b in range(NB):
        own[b] = sum_of(b, 3, table, sums)
    pl.semaphore_wait(barrier, len(peers))
    halo = []
    for f in range(2):
        halo.append((
            remote(out_hi.at[f], in_lo.at[f], hs.at[0, f], hr.at[0, f], above),
            remote(out_lo.at[f], in_hi.at[f], hs.at[1, f], hr.at[1, f], below),
        ))
    back = (
        remote(gb_hi, fb_lo, gs.at[0], gr.at[0], above),
        remote(gb_lo, fb_hi, gs.at[1], gr.at[1], below),
    )
    for copy in list(halo[1]) + list(back) + list(halo[0]):
        copy.start()

    build_picks(rmap, count[0, 0], picks)
    for b in range(NB):
        gt[b, :, 0:C] = jnp.transpose(og[b])
    scatter_grads(picks, gt, ht)

    def extend(f, own, ext):
        ext[0:NB] = own
        halo[f][0].wait()
        ext[NB : NB + KB] = jnp.where(has_below, in_lo[f], jnp.zeros_like(in_lo[f]))
        halo[f][1].wait()
        ext[NB + KB :] = jnp.where(has_above, in_hi[f], jnp.zeros_like(in_hi[f]))

    keep = pl.ds(pl.multiple_of(core * half, half), half)
    away = pl.ds(pl.multiple_of((1 - core) * half, half), half)
    chunks = [pl.ds(pl.multiple_of(own_part[g] * parts[g], parts[g]), parts[g]) for g in range(2)]
    outs = (g1_ref, g2_ref)

    def swap_halves(g):
        snd0[g] = dwp[g, away, :].astype(BF16)
        remote(snd0.at[g], rcv0.at[g], s0.at[g], r0.at[g], other).start()

    def scatter_plane(g):
        wait_all(rcv0.at[g], r0.at[g])
        snd1[g] = (dwp[g, keep, :] + rcv0[g].astype(F32)).astype(BF16)
        part = parts[g]
        for s, (index, peer) in enumerate(zip(*planes[g])):
            rows = pl.ds(pl.multiple_of(index * part, part), part)
            remote(snd1.at[g, rows, :], rcv1.at[g, s, 0:part], s1.at[g], r1.at[g], peer).start()
        at = pl.ds(pl.multiple_of(core * half + own_part[g] * part, part), part)
        mine[g, 0:part] = dwp[g, at, :] + rcv0[g, chunks[g], :].astype(F32)

    def exchange_line(g):
        part = parts[g]
        near = half // part - 1
        wait_all(rcv1.at[g, 0:near, 0:part], r1.at[g])
        total = mine[g, 0:part]
        for s in range(near):
            total = total + rcv1[g, s, 0:part].astype(F32)
        gat3[g, own_slot[g], 0:part] = total.astype(BF16)
        for peer in lines[g]:
            block = gat3.at[g, own_slot[g], 0:part]
            remote(block, block, s3.at[g], r3.at[g], peer).start()

    def gather_plane(g):
        part = parts[g]
        wait_all(gat3.at[g, 0 : slots[g] - 1, 0:part], r3.at[g])
        total = gat3[g, 0, 0:part].astype(F32)
        for i in range(1, slots[g]):
            total = total + gat3[g, i, 0:part].astype(F32)
        fin1[g, chunks[g], :] = total.astype(BF16)
        block = fin1.at[g, chunks[g], :]
        for peer in planes[g][1]:
            remote(block, block, s5.at[g], r5.at[g], peer).start()

    def share_halves(g):
        wait_all(fin1.at[g, 0 : half - parts[g]], r5.at[g])
        remote(fin1.at[g], outs[g].at[keep, :], s6.at[g], r6.at[g], other).start()
        outs[g][keep, :] = fin1[g]

    def settle(g):
        wait_all(rcv0.at[g], s0.at[g])
        wait_all(snd1.at[g, 0 : half - parts[g]], s1.at[g])
        wait_all(gat3.at[g, 0 : slots[g] - 1, 0 : parts[g]], s3.at[g])
        wait_all(fin1.at[g, 0 : half - parts[g]], s5.at[g])
        wait_all(fin1.at[g], s6.at[g])
        wait_all(fin1.at[g], r6.at[g])

    def add_back(b, total, lo, hi):
        for j in range(KB):
            from_below = jnp.where(jnp.logical_and(slo[0, j] == b, has_below), 1.0, 0.0)
            from_above = jnp.where(jnp.logical_and(shi[0, j] == b, has_above), 1.0, 0.0)
            total = total + from_below * lo[j].astype(F32) + from_above * hi[j].astype(F32)
        return total

    extend(1, feat[...], ext_x)
    gather_rows(picks, pin, ext_x, gathered)
    for copy in back:
        copy.wait()
    for b in range(NB):
        hidden_grad = add_back(b, own[b], fb_lo, fb_hi)
        gt[b, :, 0:C] = jnp.transpose(jnp.where(pre[b] > 0, hidden_grad, 0.0).astype(BF16))
    running_sums(
        lambda p: jnp.dot(gathered[p], gt[p // PB], preferred_element_type=F32), 0, poff, table, sums
    )
    pack(table, sums, dwp.at[0])
    swap_halves(0)

    extend(0, jnp.maximum(pre[...], 0.0), ext_h)
    running_sums(
        lambda p: jnp.dot(ext_h[pin[0, p]], ht[p], preferred_element_type=F32), 0, poff, table, sums
    )
    pack(table, sums, dwp.at[1])
    swap_halves(1)
    scatter_plane(0)
    scatter_plane(1)

    scatter_grads(picks, gt, ht)
    loads["w1"].wait()
    running_sums(
        lambda p: lax.dot_general(w1[poff[0, p]], ht[p, :, 0:C], NT, preferred_element_type=F32),
        3, pin, table, sums,
    )
    for j in range(KB):
        gb2_lo[j] = sum_of(NB + j, 3, table, sums)
        gb2_hi[j] = sum_of(NB + KB + j, 3, table, sums)
    for b in range(NB):
        own[b] = sum_of(b, 3, table, sums)

    exchange_line(0)
    exchange_line(1)
    last = (
        remote(gb2_hi, fb2_lo, g2s.at[0], g2r.at[0], above),
        remote(gb2_lo, fb2_hi, g2s.at[1], g2r.at[1], below),
    )
    for copy in last:
        copy.start()
    gather_plane(0)
    gather_plane(1)
    for copy in last:
        copy.wait()
    for b in range(NB):
        fg_ref[b] = add_back(b, own[b], fb2_lo, fb2_hi).astype(BF16)
    share_halves(0)
    share_halves(1)
    settle(0)
    settle(1)


def fused(ny, nz, nx, *operands):
    half = PACKED // 2
    part = half // (min(ny, nz) * nx)
    most = max(ny, nz)
    near = most * nx - 1
    dma = pltpu.SemaphoreType.DMA
    packed = jax.ShapeDtypeStruct((PACKED, ROW), BF16)
    blocks = jax.ShapeDtypeStruct((NB, C, ROW), BF16)
    four = pltpu.VMEM((NB, C, ROW), BF16)
    four_wide = pltpu.VMEM((NB, C, ROW), F32)
    kernel_weights = pltpu.VMEM((K, C, C), BF16)
    return pl.pallas_call(
        functools.partial(fused_kernel, ny, nz, nx),
        out_shape=(packed, packed, blocks),
        in_specs=[HBM] * 11,
        out_specs=(VMEM,) * 3,
        scratch_shapes=[
            four, four, four, kernel_weights, kernel_weights,
            pltpu.VMEM((1, PAIRS, ROW), jnp.int32),
            pltpu.VMEM((1, PAIRS), jnp.int32),
            pltpu.VMEM((1, PAIRS), jnp.int32),
            pltpu.SMEM((1, 1), jnp.int32),
            pltpu.SMEM((1, PAIRS), jnp.int32),
            pltpu.SMEM((1, PAIRS), jnp.int32),
            pltpu.SMEM((1, KB), jnp.int32),
            pltpu.SMEM((1, KB), jnp.int32),
            pltpu.VMEM((8, ROW), jnp.int32),
            pltpu.SMEM((8, ROW), jnp.int32),
            pltpu.VMEM((PAIRS, ROW, ROW), BF16),
            pltpu.VMEM((NB, ROW, ROW), BF16),
            pltpu.VMEM((PAIRS, ROW, ROW), BF16),
            pltpu.VMEM((PAIRS, C, ROW), BF16),
            pltpu.VMEM((PAIRS, C, ROW), F32),
            pltpu.VMEM((EXT, C, ROW), BF16),
            pltpu.VMEM((EXT, C, ROW), BF16),
            four_wide,
            pltpu.VMEM((2, KB, C, ROW), BF16),
            pltpu.VMEM((2, KB, C, ROW), BF16),
            pltpu.VMEM((2, KB, C, ROW), BF16),
            pltpu.VMEM((2, KB, C, ROW), BF16),
            four, four, four, four, four_wide, four_wide, four_wide, four_wide,
            pltpu.VMEM((2, PACKED, ROW), F32),
            pltpu.VMEM((2, half, ROW), BF16),
            pltpu.VMEM((2, half, ROW), BF16),
            pltpu.VMEM((2, half, ROW), BF16),
            pltpu.VMEM((2, near, part, ROW), BF16),
            pltpu.VMEM((2, part, ROW), F32),
            pltpu.VMEM((2, most, part, ROW), BF16),
            pltpu.VMEM((2, half, ROW), BF16),
            dma((13,)), dma,
            dma((2, 2)), dma((2, 2)),
            dma((2,)), dma((2,)),
            dma((2,)), dma((2,)),
            dma((2,)), dma((2,)),
            dma((2,)), dma((2,)),
            dma((2,)), dma((2,)),
            dma((2,)), dma((2,)),
            dma((2,)), dma((2,)),
        ],
        compiler_params=pltpu.CompilerParams(
            collective_id=0, has_side_effects=True, vmem_limit_bytes=VMEM_LIMIT
        ),
        name="fused",
    )(*operands)


def finish_kernel(grad_ref, g1_ref, g2_ref, fg_ref, w1_ref, w2_ref, wide, sems, last):
    lane = lax.broadcasted_iota(jnp.int32, (C, ROW), 1)
    first = pltpu.make_async_copy(grad_ref, fg_ref, last)
    first.start()
    copies = [first]
    for g, (src, dst) in enumerate(((g1_ref, w1_ref), (g2_ref, w2_ref))):
        for q in range(7):
            base = q * 3 * C
            size = min(4, K - 4 * q)
            r1 = src[base : base + C, :].astype(F32)
            r2 = src[base + C : base + 2 * C, :].astype(F32)
            r3 = src[base + 2 * C : base + 3 * C, :].astype(F32)
            wide[g, 4 * q] = r1[:, 0:C]
            wide[g, 4 * q + 1] = pltpu.roll(jnp.where(lane < 96, r2, r1), 32, 1)[:, 0:C]
            wide[g, 4 * q + 2] = pltpu.roll(jnp.where(lane < 64, r3, r2), 64, 1)[:, 0:C]
            if size == 4:
                wide[g, 4 * q + 3] = pltpu.roll(r3, 96, 1)[:, 0:C]
            copy = pltpu.make_async_copy(
                wide.at[g, pl.ds(4 * q, size)], dst.at[pl.ds(4 * q, size)], sems.at[g, q]
            )
            copy.start()
            copies.append(copy)
    for copy in copies:
        copy.wait()


def finish(grad, g1, g2):
    kern = jax.ShapeDtypeStruct((K, C, C), F32)
    return pl.pallas_call(
        finish_kernel,
        out_shape=(jax.ShapeDtypeStruct((NB, C, ROW), BF16), kern, kern),
        in_specs=[VMEM] * 3,
        out_specs=(HBM,) * 3,
        scratch_shapes=[
            pltpu.VMEM((2, K, C, C), F32),
            pltpu.SemaphoreType.DMA((2, 7)),
            pltpu.SemaphoreType.DMA,
        ],
        compiler_params=pltpu.CompilerParams(vmem_limit_bytes=VMEM_LIMIT),
        name="finish",
    )(grad, g1, g2)


def body(ny, nz, nx, features, pre_act, out_grad, weight_one, weight_two, block_count, pair_in, pair_off,
         row_map, send_lo, send_hi):
    operands = (features, pre_act, out_grad, weight_one, weight_two, block_count.reshape(1, 1), pair_in, pair_off,
                row_map, send_lo, send_hi)
    operands = [a if a.size == 1 else pltpu.with_memory_space_constraint(a, pltpu.HBM) for a in operands]
    g1, g2, grad = fused(ny, nz, nx, *operands)
    return finish(grad, g1, g2)


def solution(mesh):
    placed = (
        P(("district", "tile"), None, None),
        P(("district", "tile"), None, None),
        P(("district", "tile"), None, None),
        P(),
        P(),
        P(("district", "tile")),
        P(("district", "tile"), None),
        P(("district", "tile"), None),
        P(("district", "tile"), None, None),
        P(("district", "tile"), None),
        P(("district", "tile"), None),
    )
    tiles = mesh.shape["tile"]
    nx = 4 if tiles % 4 == 0 and tiles > 4 else 2
    ny, nz = mesh.shape["district"] // 2, tiles // nx
    return jax.shard_map(
        functools.partial(body, ny, nz, nx),
        mesh=mesh,
        in_specs=placed,
        out_specs=(P(("district", "tile"), None, None), P(), P()),
        check_vma=False,
    )
```
